256 devices in a mesh: row: 8 (over y, z_lo), col: 8 (over z_hi, core), kern: 4 (over x).
Axes of the slice: x: 4, y: 4, z: 8 (z_hi: 4, z_lo: 2; z = z_hi * 2 + z_lo), core: 2. Of those that a mesh axis runs over, the one named last changes fastest.
Arguments:
- photomask: float32 [2048, 2048], P('row', 'col'), may hold values from 0 to 1
- target_bits: int32 [2048, 2048], P('row', 'col'), may hold values 0 or 1
- active_blocks: int32 [32, 32], P('row', 'col'), may hold values 0 or 1
- kernel_taps: float32 [2, 12, 257, 257], P(None, 'kern'), may hold values from -0.0234375 to 0.0234375
- kernel_weights: float32 [12], P('kern'), may hold values from 0.1 to 1
Outputs:
- gradient: float32 [2048, 2048], P(('row', 'kern'), 'col')
- resist: float32 [2048, 2048], P('row', 'col')
The draws below stay inside these ranges and needn't reach their ends.
All inputs are finite; a program needn't handle non-finite values. No bound on the sum of `target_bits` or of `active_blocks` on one device may be relied on, other than what follows from the above.
Results may differ from the reference program's by a relative error of at most 0.00011.
Values sent between devices are 32-bit elements; how exact they have to be, the bound alone decides.
A program may use at most 128 MiB of HBM per device.

```python
import math
import jax
import jax.numpy as jnp

RAD = 128
KS = 257
KERNELS = 12
BLK = 64
NX = 2048
NY = 2048


def touch_ends(array, stream_key, smallest, largest):
    dims = array.shape
    place = [jax.random.randint(jax.random.fold_in(stream_key, axis), (), 0, dims[axis]) for axis in range(len(dims))]
    array = array.at[tuple(place)].set(smallest)
    longest = dims.index(max(dims))
    place[longest] = (place[longest] + 1) % dims[longest]
    return array.at[tuple(place)].set(largest)


def levels(stream_key, dims, shards, low, top_value):
    factor_of, own = 1.0, jax.random.fold_in(stream_key, 6)
    for axis_at, shards_of in shards:
        steps = jnp.exp(jax.random.uniform(jax.random.fold_in(own, axis_at), (shards_of,), jnp.float32, low / len(shards), top_value / len(shards)))
        factor_of = factor_of * jnp.repeat(steps, dims[axis_at] // shards_of).reshape([-1 if axis == axis_at else 1 for axis in range(len(dims))])
    return factor_of


def centred(rng, extent, deviation, bound, split=(), kind=jnp.bfloat16):
    entries = jax.random.normal(rng, extent, jnp.float32) * deviation
    if len(split) > 0:
        entries = levels(rng, extent, split, -0.22, 0.18) * entries
    return jnp.clip(entries, min=-bound, max=bound).astype(kind)


def setup_inputs(seed: int = 0) -> dict:
    keys = jax.random.split(jax.random.key(seed), 6)
    photomask = jnp.clip(1.0 * jax.random.uniform(keys[0], (NX, NY), jnp.float32) ** levels(keys[0], (NX, NY), ((0, 8), (1, 8)), -0.2, 0.2), 0.0, 1.0)
    target_bits = touch_ends((jax.random.randint(keys[1], (NX, NY), 0, 2) < 1).astype(jnp.int32), jax.random.fold_in(keys[1], 1), 0, 1)
    active_blocks = touch_ends((jax.random.randint(keys[2], (NX // BLK, NY // BLK), 0, 4) < 3).astype(jnp.int32), jax.random.fold_in(keys[2], 1), 0, 1)
    kernel_taps = centred(keys[3], (2, KERNELS, KS, KS), (KS * KS) ** -0.5, 0.0234375, ((1, 4),), jnp.float32)
    kernel_weights = jnp.clip(jnp.exp(math.log(1.0) - 2.3025851 * jax.random.uniform(keys[4], (KERNELS,), jnp.float32) ** levels(keys[4], (KERNELS,), ((0, 4),), -0.2, 0.2)), 0.1, 1.0)
    return {"photomask": photomask, "target_bits": target_bits, "active_blocks": active_blocks, "kernel_taps": kernel_taps, "kernel_weights": kernel_weights}


steepness = 8.0
threshold = 0.25


def embed(taps, rows, cols):
    placed = jnp.pad(taps, ((0, rows - KS), (0, cols - KS)))
    return jnp.roll(placed, (-RAD, -RAD), (0, 1))


def reference(photomask, target_bits, active_blocks, kernel_taps, kernel_weights):
    rows = NX + 2 * RAD
    cols = NY + 2 * RAD
    mask_spectrum = jnp.fft.rfft2(jnp.pad(photomask, RAD))
    spectra = []
    amplitudes = []
    intensity = jnp.zeros((NX, NY), jnp.float32)
    for kernel_index in range(KERNELS):
        pair_spectra = []
        pair_fields = []
        for part_index in range(2):
            spectrum = jnp.fft.rfft2(embed(kernel_taps[part_index, kernel_index], rows, cols))
            field = jnp.fft.irfft2(mask_spectrum * jnp.conj(spectrum), s=(rows, cols))[RAD:RAD + NX, RAD:RAD + NY]
            pair_spectra.append(spectrum)
            pair_fields.append(field)
        spectra.append(pair_spectra)
        amplitudes.append(pair_fields)
        intensity = intensity + kernel_weights[kernel_index] * (pair_fields[0] * pair_fields[0] + pair_fields[1] * pair_fields[1])
    intensity = intensity / KERNELS
    resist = jax.nn.sigmoid(steepness * (intensity - threshold))
    factor = 2.0 * (resist - target_bits.astype(jnp.float32)) * steepness * resist * (1.0 - resist)
    total = None
    for kernel_index in range(KERNELS):
        for part_index in range(2):
            product = factor * (2.0 / KERNELS) * kernel_weights[kernel_index] * amplitudes[kernel_index][part_index]
            term = jnp.fft.rfft2(jnp.pad(product, RAD)) * spectra[kernel_index][part_index]
            total = term if total is None else total + term
    gradient = jnp.fft.irfft2(total, s=(rows, cols))[RAD:RAD + NX, RAD:RAD + NY]
    pixels = jnp.repeat(jnp.repeat(active_blocks, BLK, 0), BLK, 1).astype(jnp.float32)
    return gradient * pixels, resist
```

```python
import functools

import jax
import jax.numpy as jnp
import numpy as np
from jax import lax
from jax.experimental import pallas as pl
from jax.experimental.pallas import tpu as pltpu
from jax.sharding import PartitionSpec as P

MESH = pl.DeviceIdType.MESH
T = 256
W = 512
R = 128
PARTS = 6
Q = 64
SCALE = 2.0 ** -17
F32 = jnp.float32
BF = jnp.bfloat16


def tables():
    sample = np.arange(W)[:, None]
    freq = np.arange(T)[None, :]
    angle = np.pi / W * (sample * (2 * freq + 1) % (2 * W))
    cos, sin = np.cos(angle), np.sin(angle)
    full = np.concatenate([cos[:, :R], sin[:, :R], cos[:, R:], sin[:, R:]], axis=1)
    full[np.abs(full) < 1e-12] = 0.0
    high = full.astype(BF)
    low = (full - high.astype(np.float64)).astype(BF)
    return high, low, np.ascontiguousarray(high.T), np.ascontiguousarray(low.T)


def split(value):
    high = value.astype(BF)
    return high, (value - high.astype(F32)).astype(BF)


def dot(a, b):
    return jnp.dot(a, b, preferred_element_type=F32)


def dot3(ah, al, bh, bl):
    return dot(ah, bh) + dot(al, bh) + dot(ah, bl)


def to_complex(block):
    cc, cs = block[:R, :R], block[:R, R:]
    sc, ss = block[R:, :R], block[R:, R:]
    return cc - ss, -(cs + sc), cc + ss, cs - sc


def from_complex(pr, pi, mr, mi):
    return pr + mr, mi - pi, -(pi + mi), mr - pr


def kernel(
    mask, target, active, taps, weights, rh_in, rl_in, th_in, tl_in,
    gradient, resist,
    win, tapv, rh, rl, th, tl, targ, taph, rhat, xh, xl, hs, ms, vh, vl, amp, ph, pw,
    ipart, irecv, resv, acc, tsend, trecv, fsend, frecv, gw, erecv, outv,
    lsem, msend, mrecv, isend, isem, asend, asem, tss, trs, fss, frs, ess, ers,
):
    r, c, j = lax.axis_index("row"), lax.axis_index("col"), lax.axis_index("kern")
    rows, cols = lax.axis_size("row"), lax.axis_size("col")
    has = (r > 0, r < rows - 1, c > 0, c < cols - 1)
    where = ({"row": r - 1}, {"row": r + 1}, {"col": c - 1}, {"col": c + 1})
    peer = [lax.rem(j + d, 4) for d in range(4)]

    loads = [
        pltpu.make_async_copy(mask, win.at[R:R + T, R:R + T], lsem.at[0]),
        pltpu.make_async_copy(taps, tapv, lsem.at[1]),
        pltpu.make_async_copy(rh_in, rh, lsem.at[2]),
        pltpu.make_async_copy(rl_in, rl, lsem.at[3]),
        pltpu.make_async_copy(th_in, th, lsem.at[4]),
        pltpu.make_async_copy(tl_in, tl, lsem.at[5]),
        pltpu.make_async_copy(target, targ, lsem.at[6]),
    ]
    for load in loads:
        load.start()

    @pl.when(r == 0)
    def _():
        win[:R, :] = jnp.zeros((R, W), F32)

    @pl.when(r == rows - 1)
    def _():
        win[R + T:, :] = jnp.zeros((R, W), F32)

    @pl.when(c == 0)
    def _():
        win[:, :R] = jnp.zeros((W, R), F32)

    @pl.when(c == cols - 1)
    def _():
        win[:, R + T:] = jnp.zeros((W, R), F32)

    barrier = pltpu.get_barrier_semaphore()
    for i in range(4):
        @pl.when(has[i])
        def _(i=i):
            pl.semaphore_signal(barrier, inc=1, device_id=where[i], device_id_type=MESH)
    for d in range(1, 4):
        pl.semaphore_signal(barrier, inc=1, device_id={"kern": peer[d]}, device_id_type=MESH)
    count = 3
    for i in range(4):
        count = count + has[i].astype(jnp.int32)
    pl.semaphore_wait(barrier, count)

    def remote(src, dst, s, d, to):
        return pltpu.make_async_remote_copy(
            src_ref=src, dst_ref=dst, send_sem=s, recv_sem=d, device_id=to, device_id_type=MESH)

    low, mid, high = slice(0, R), slice(R, R + T), slice(R + T, W)
    first, second = slice(R, 2 * R), slice(2 * R, 3 * R)
    halo = [
        (0, mask.at[0:R, :], win.at[high, mid], 1),
        (1, mask.at[R:T, :], win.at[low, mid], 0),
        (2, mask.at[:, 0:R], win.at[mid, high], 3),
        (3, mask.at[:, R:T], win.at[mid, low], 2),
        (2, win.at[low, first], win.at[low, high], 6),
        (2, win.at[high, first], win.at[high, high], 7),
        (3, win.at[low, second], win.at[low, low], 4),
        (3, win.at[high, second], win.at[high, low], 5),
    ]
    copies = [remote(s, d, msend.at[k], mrecv.at[k], where[i]) for i, s, d, k in halo]
    back = (1, 0, 3, 2)

    def on(side, fn):
        pl.when(has[side])(fn)

    for n in range(4):
        on(halo[n][0], copies[n].start)

    for load in loads[1:6]:
        load.wait()
    sign_row = (1 - 2 * (lax.broadcasted_iota(jnp.int32, (1, R), 1) & 1)).astype(F32)
    sign_col = (1 - 2 * (lax.broadcasted_iota(jnp.int32, (R, 1), 0) & 1)).astype(F32)
    taph[...] = jnp.zeros_like(taph)
    for a in range(PARTS):
        taph[a:a + 1, :] = tapv[a // 3, a % 3, T:T + 1, 0:T]
    edge_h, edge_l = split(taph[...])
    rhat[...] = dot3(edge_h, edge_l, rh[:T, :], rl[:T, :])
    for a in range(PARTS):
        corner = tapv[a // 3, a % 3, T:T + 1, T:T + 1]
        for b in range(2):
            at = slice(b * T + R, b * T + T)
            rhat[a:a + 1, at] = rhat[a:a + 1, at] + corner * sign_row

    def tap_spectrum(a, carry):
        part, k = a // 3, lax.rem(a, 3)
        low_h, low_l = split(tapv[part, k, 0:T, 0:T])
        column = tapv[part, k, 0:T, T:T + 1]
        for b in range(2):
            at = slice(b * T, b * T + T)
            value = dot3(low_h, low_l, rh[:T, at], rl[:T, at])
            value = jnp.concatenate([value[:, :R], value[:, R:] + column * sign_row], axis=1)
            vh_, vl_ = split(value)
            xh[:T, at] = vh_
            xl[:T, at] = vl_
        for b in range(2):
            at = slice(b * T, b * T + T)
            value = dot3(th[:, :T], tl[:, :T], xh[:T, at], xl[:T, at])
            edge = sign_col * rhat[pl.ds(a, 1), at]
            for f in range(2):
                block = value[f * T:f * T + T]
                block = jnp.concatenate([block[:R], block[R:] + edge], axis=0)
                for n, x in enumerate(to_complex(block)):
                    hs[a, n, f * R:f * R + R, b * R:b * R + R] = x
        return carry

    lax.fori_loop(0, 3, tap_spectrum, 0)

    loads[0].wait()
    for n in range(2):
        on(back[halo[n][0]], copies[n].wait_recv)
    for n in range(4, 8):
        on(halo[n][0], copies[n].start)

    lax.fori_loop(3, PARTS, tap_spectrum, 0)

    for n in range(2, 8):
        on(back[halo[n][0]], copies[n].wait_recv)

    for half in range(2):
        up = slice(half * T, half * T + T)
        wh_, wl_ = split(win[up, :])
        for b in range(2):
            at = slice(b * T, b * T + T)
            h_, l_ = split(dot3(wh_, wl_, rh[:, at], rl[:, at]))
            xh[up, at] = h_
            xl[up, at] = l_
    for b in range(2):
        at = slice(b * T, b * T + T)
        value = dot3(th[...], tl[...], xh[:, at], xl[:, at])
        for f in range(2):
            for n, x in enumerate(to_complex(value[f * T:f * T + T])):
                ms[n, f * R:f * R + R, b * R:b * R + R] = x

    def inverse_rows(a, carry):
        for b in range(2):
            for f in range(2):
                at = (slice(f * R, f * R + R), slice(b * R, b * R + R))
                m = [ms[n, at[0], at[1]] for n in range(4)]
                h = [hs[a, n, at[0], at[1]] for n in range(4)]
                y = []
                for n in (0, 2):
                    y.append(m[n] * h[n] + m[n + 1] * h[n + 1])
                    y.append(m[n + 1] * h[n] - m[n] * h[n + 1])
                for n, x in enumerate(from_complex(*y)):
                    h_, l_ = split(x)
                    to = (slice(f * T + (n // 2) * R, f * T + (n // 2) * R + R),
                          slice(b * T + (n % 2) * R, b * T + (n % 2) * R + R))
                    xh[to[0], to[1]] = h_
                    xl[to[0], to[1]] = l_
            at = slice(b * T, b * T + T)
            h_, l_ = split(dot3(rh[:T, :], rl[:T, :], xh[:, at], xl[:, at]))
            vh[a, :, at] = h_
            vl[a, :, at] = l_
        return carry

    lax.fori_loop(0, PARTS, inverse_rows, 0)

    def share_rows(q):
        return pl.ds(pl.multiple_of(q * Q, Q), Q)

    def share_amplitude(d):
        at = share_rows(peer[d])
        value = dot3(vh[:, at, :].reshape(PARTS * Q, W), vl[:, at, :].reshape(PARTS * Q, W),
                     th[:, :T], tl[:, :T]).reshape(PARTS, Q, T) * SCALE
        amp[:, at, :] = value
        total = None
        for k in range(3):
            term = weights[k] * (value[k] * value[k] + value[k + 3] * value[k + 3])
            total = term if total is None else total + term
        return total

    sums = []
    for d in range(1, 4):
        ipart[d - 1] = share_amplitude(d)
        copy = remote(ipart.at[d - 1], irecv.at[d - 1], isend.at[d - 1], isem.at[d - 1], {"kern": peer[d]})
        copy.start()
        sums.append(copy)
    total = share_amplitude(0)
    for copy in sums:
        copy.wait_recv()
    intensity = (total + irecv[0] + irecv[1] + irecv[2]) * (1.0 / 12.0)
    own = share_rows(j)
    resv[own, :] = 1.0 / (1.0 + jnp.exp(-8.0 * (intensity - 0.25)))
    shares = []
    for d in range(1, 4):
        copy = remote(resv.at[own, :], resv.at[own, :], asend.at[d - 1], asem.at[d - 1], {"kern": peer[d]})
        copy.start()
        shares.append(copy)

    loads[6].wait()

    def share_product(q):
        at = share_rows(q)
        x = resv[at, :]
        factor = 2.0 * (x - targ[at, :].astype(F32)) * 8.0 * x * (1.0 - x)
        both = [split(factor * (weights[a % 3] * (2.0 / 12.0)) * amp[a, at, :]) for a in range(PARTS)]
        h_ = jnp.concatenate([x[0] for x in both], axis=0)
        l_ = jnp.concatenate([x[1] for x in both], axis=0)
        for b in range(2):
            cut = slice(b * T, b * T + T)
            u, v = split(dot3(h_, l_, rh[:T, cut], rl[:T, cut]).reshape(PARTS, Q, T))
            ph[:, at, cut] = u
            pw[:, at, cut] = v

    share_product(j)
    for d in range(1, 4):
        q = lax.rem(j + 4 - d, 4)
        rows_q = share_rows(q)
        remote(resv.at[rows_q, :], resv.at[rows_q, :], asend.at[d - 1], asem.at[d - 1],
               {"kern": peer[d]}).wait_recv()
        share_product(q)
    store = pltpu.make_async_copy(resv, resist, lsem.at[7])
    store.start()

    windows = []
    for b in range(2):
        at = slice(b * T, b * T + T)
        acc[...] = jnp.zeros_like(acc)

        def gather(a, carry, at=at, b=b):
            value = dot3(th[:, :T], tl[:, :T], ph[a, :, at], pw[a, :, at])
            for f in range(2):
                p = to_complex(value[f * T:f * T + T])
                fr = slice(f * R, f * R + R)
                h = [hs[a, n, fr, b * R:b * R + R] for n in range(4)]
                for n in (0, 2):
                    acc[n, fr, :] += p[n] * h[n] - p[n + 1] * h[n + 1]
                    acc[n + 1, fr, :] += p[n] * h[n + 1] + p[n + 1] * h[n]
            return carry

        lax.fori_loop(0, PARTS, gather, 0)
        for f in range(2):
            fr = slice(f * R, f * R + R)
            for n, x in enumerate(from_complex(*[acc[i, fr, :] for i in range(4)])):
                h_, l_ = split(x)
                to = (slice(f * T + (n // 2) * R, f * T + (n // 2) * R + R),
                      slice(b * T + (n % 2) * R, b * T + (n % 2) * R + R))
                xh[to[0], to[1]] = h_
                xl[to[0], to[1]] = l_
        tsend[b] = dot3(rh[...], rl[...], xh[:, at], xl[:, at]).reshape(8, Q, T)
        for far in range(2):
            for d in range(1, 4):
                chunk = lax.rem(peer[d] + 6, 8) if far == 0 else peer[d] + 2
                n = (b * 2 + far) * 3 + d - 1
                copy = remote(tsend.at[b, chunk], trecv.at[n], tss.at[n], trs.at[n], {"kern": peer[d]})
                copy.start()
                windows.append(copy)

    def summed(b, far):
        n = (b * 2 + far) * 3
        for d in range(3):
            windows[n + d].wait_recv()
        chunk = lax.rem(j + 6, 8) if far == 0 else j + 2
        return tsend[b, chunk] + trecv[n] + trecv[n + 1] + trecv[n + 2]

    down = j < 2
    step = jnp.where(down, 1, -1)
    gives = jnp.logical_or(jnp.logical_and(down, has[1]), jnp.logical_and(jnp.logical_not(down), has[0]))
    takes = jnp.logical_or(jnp.logical_and(down, has[0]), jnp.logical_and(jnp.logical_not(down), has[1]))
    hops = [remote(fsend.at[b], frecv.at[b], fss.at[b], frs.at[b], {"row": r + step}) for b in range(2)]
    near = []
    for b in range(2):
        fsend[b] = summed(b, 0)
        pl.when(gives)(hops[b].start)
        near.append(summed(b, 1))
    for b in range(2):
        gw[:, b * T:b * T + T] = near[b]
    for b in range(2):
        @pl.when(takes)
        def _(b=b):
            hops[b].wait_recv()
            at = slice(b * T, b * T + T)
            gw[:, at] = gw[:, at] + frecv[b]
    g_h, g_l = split(gw[...])
    gw[...] = dot3(g_h, g_l, th[...], tl[...])
    ends = [
        remote(gw.at[:, low], erecv.at[1], ess.at[1], ers.at[1], {"col": c - 1}),
        remote(gw.at[:, high], erecv.at[0], ess.at[0], ers.at[0], {"col": c + 1}),
    ]
    on(2, ends[0].start)
    on(3, ends[1].start)
    lane = lax.broadcasted_iota(jnp.int32, (1, T), 1) // 64
    pixels = jnp.zeros((1, T), F32)
    for k in range(4):
        pixels = jnp.where(lane == k, active[j, k].astype(F32), pixels)
    pixels = pixels * SCALE

    for n, side, cut in ((1, 2, slice(0, R)), (0, 3, slice(R, T))):
        from_cut = slice(cut.start + R, cut.stop + R)

        @pl.when(has[side])
        def _(n=n, side=side, cut=cut, from_cut=from_cut):
            ends[n].wait_recv()
            outv[:, cut] = (gw[:, from_cut] + erecv[side - 2]) * pixels[:, cut]

        @pl.when(jnp.logical_not(has[side]))
        def _(cut=cut, from_cut=from_cut):
            outv[:, cut] = gw[:, from_cut] * pixels[:, cut]

    final = pltpu.make_async_copy(outv, gradient, lsem.at[0])
    final.start()

    for n in range(8):
        on(halo[n][0], copies[n].wait_send)
    for copy in sums + shares + windows:
        copy.wait_send()
    for b in range(2):
        pl.when(gives)(hops[b].wait_send)
    on(2, ends[0].wait_send)
    on(3, ends[1].wait_send)
    store.wait()
    final.wait()


def local(photomask, target_bits, active_blocks, kernel_taps, kernel_weights):
    hbm = pl.BlockSpec(memory_space=pl.ANY)
    smem = pl.BlockSpec(memory_space=pltpu.SMEM)
    vmem = pltpu.VMEM
    dma = pltpu.SemaphoreType.DMA
    scratch = [
        vmem((W, W), F32),
        vmem((2, 3, 2 * R + 1, 2 * R + 1), F32),
        vmem((W, W), BF), vmem((W, W), BF), vmem((W, W), BF), vmem((W, W), BF),
        vmem((T, T), jnp.int32),
        vmem((8, T), F32),
        vmem((8, W), F32),
        vmem((W, W), BF), vmem((W, W), BF),
        vmem((PARTS, 4, T, T), F32),
        vmem((4, T, T), F32),
        vmem((PARTS, T, W), BF), vmem((PARTS, T, W), BF),
        vmem((PARTS, T, T), F32),
        vmem((PARTS, T, W), BF), vmem((PARTS, T, W), BF),
        vmem((3, Q, T), F32), vmem((3, Q, T), F32),
        vmem((T, T), F32),
        vmem((4, T, R), F32),
        vmem((2, 8, Q, T), F32),
        vmem((12, Q, T), F32),
        vmem((2, Q, T), F32), vmem((2, Q, T), F32),
        vmem((Q, W), F32),
        vmem((2, Q, R), F32),
        vmem((Q, T), F32),
        dma((8,)), dma((8,)), dma((8,)),
        dma((3,)), dma((3,)), dma((3,)), dma((3,)),
        dma((12,)), dma((12,)),
        dma((2,)), dma((2,)), dma((2,)), dma((2,)),
    ]
    return pl.pallas_call(
        kernel,
        out_shape=(jax.ShapeDtypeStruct((Q, T), F32), jax.ShapeDtypeStruct((T, T), F32)),
        in_specs=[hbm, hbm, smem, hbm, smem, hbm, hbm, hbm, hbm],
        out_specs=(hbm, hbm),
        scratch_shapes=scratch,
        compiler_params=pltpu.CompilerParams(
            collective_id=0, has_side_effects=True, vmem_limit_bytes=56 * 1024 * 1024),
        name="socs",
    )(photomask, target_bits, active_blocks, kernel_taps, kernel_weights, *[jnp.asarray(t) for t in tables()])


def solution(mesh):
    in_specs = (
        P("row", "col"),
        P("row", "col"),
        P("row", "col"),
        P(None, "kern", None, None),
        P("kern"),
    )
    out_specs = (P(("row", "kern"), "col"), P("row", "col"))
    return jax.shard_map(local, mesh=mesh, in_specs=in_specs, out_specs=out_specs, check_vma=False)
```

```python
import functools

import jax
import jax.numpy as jnp
import numpy as np
from jax import lax
from jax.experimental import pallas as pl
from jax.experimental.pallas import tpu as pltpu
from jax.sharding import PartitionSpec as P

MESH = pl.DeviceIdType.MESH
T = 256
W = 512
R = 128
PARTS = 6
Q = 64
SCALE = 2.0 ** -17
F32 = jnp.float32
BF = jnp.bfloat16


def tables():
    sample = np.arange(W)[:, None]
    freq = np.arange(T)[None, :]
    angle = np.pi / W * (sample * (2 * freq + 1) % (2 * W))
    cos, sin = np.cos(angle), np.sin(angle)
    full = np.concatenate([cos[:, :R], sin[:, :R], cos[:, R:], sin[:, R:]], axis=1)
    full[np.abs(full) < 1e-12] = 0.0
    high = full.astype(BF)
    low = (full - high.astype(np.float64)).astype(BF)
    return high, low, np.ascontiguousarray(high.T), np.ascontiguousarray(low.T)


def split(value):
    high = value.astype(BF)
    return high, (value - high.astype(F32)).astype(BF)


def dot(a, b):
    return jnp.dot(a, b, preferred_element_type=F32)


def dot3(ah, al, bh, bl):
    return dot(ah, bh) + dot(al, bh) + dot(ah, bl)


def to_complex(block):
    cc, cs = block[:R, :R], block[:R, R:]
    sc, ss = block[R:, :R], block[R:, R:]
    return cc - ss, -(cs + sc), cc + ss, cs - sc


def from_complex(pr, pi, mr, mi):
    return pr + mr, mi - pi, -(pi + mi), mr - pr


def hand_over(gradient, resist, gradient_out, resist_out):
    gradient_out[...] = gradient[...]
    resist_out[...] = resist[...]


def loop(lo, hi, fn, init):
    for i in range(lo, hi):
        fn(i, init)


def kernel(
    mask, target, active, taps, weights, rh_in, rl_in, th_in, tl_in,
    gradient, resist,
    win, tapv, rh, rl, th, tl, targ, taph, rhat, xh, xl, hs, ms, vh, vl, amp, ph, pw,
    ipart, irecv, resv, acc, tsend, trecv, gw, ecen, eside, outv,
    lsem, msend, mrecv, psend, precv, isend, isem, asend, asem, tss, trs, ess, ers,
):
    r, c, j = lax.axis_index("row"), lax.axis_index("col"), lax.axis_index("kern")
    rows, cols = lax.axis_size("row"), lax.axis_size("col")
    def exists(dr, dc):
        ok = None
        for at, d, n in ((r, dr, rows), (c, dc, cols)):
            if d:
                one = at > 0 if d < 0 else at < n - 1
                ok = one if ok is None else jnp.logical_and(ok, one)
        return ok

    def device(dr, dc):
        return {"row": r + dr, "col": c + dc}

    around = [(dr, dc) for dr in (-1, 0, 1) for dc in (-1, 0, 1) if dr or dc]
    down = j < 2
    step = jnp.where(down, 1, -1)
    gives = jnp.logical_or(jnp.logical_and(down, r < rows - 1), jnp.logical_and(jnp.logical_not(down), r > 0))
    takes = jnp.logical_or(jnp.logical_and(down, r > 0), jnp.logical_and(jnp.logical_not(down), r < rows - 1))
    peer = [lax.rem(j + d, 4) for d in range(4)]

    loads = [
        pltpu.make_async_copy(mask, win.at[R:R + T, R:R + T], lsem.at[0]),
        pltpu.make_async_copy(rh_in, rh, lsem.at[1]),
        pltpu.make_async_copy(rl_in, rl, lsem.at[2]),
        pltpu.make_async_copy(th_in, th, lsem.at[3]),
        pltpu.make_async_copy(tl_in, tl, lsem.at[4]),
        pltpu.make_async_copy(target, targ, lsem.at[5]),
    ]
    loads += [
        pltpu.make_async_copy(taps.at[a % 3, :, a // 3, :], tapv.at[a // 3, a % 3], lsem.at[8 + a])
        for a in range(PARTS)
    ]
    for load in loads:
        load.start()

    @pl.when(r == 0)
    def _():
        win[:R, :] = jnp.zeros((R, W), F32)

    @pl.when(r == rows - 1)
    def _():
        win[R + T:, :] = jnp.zeros((R, W), F32)

    @pl.when(c == 0)
    def _():
        win[:, :R] = jnp.zeros((W, R), F32)

    @pl.when(c == cols - 1)
    def _():
        win[:, R + T:] = jnp.zeros((W, R), F32)

    ecen[...] = jnp.zeros_like(ecen)
    eside[...] = jnp.zeros_like(eside)
    barrier = pltpu.get_barrier_semaphore()
    count = 3
    for dr, dc in around:
        ok = exists(dr, dc)
        count = count + ok.astype(jnp.int32)

        @pl.when(ok)
        def _(dr=dr, dc=dc):
            pl.semaphore_signal(barrier, inc=1, device_id=device(dr, dc), device_id_type=MESH)
    for d in range(1, 4):
        pl.semaphore_signal(barrier, inc=1, device_id={"kern": peer[d]}, device_id_type=MESH)
    pl.semaphore_wait(barrier, count)

    def remote(src, dst, s, d, to):
        return pltpu.make_async_remote_copy(
            src_ref=src, dst_ref=dst, send_sem=s, recv_sem=d, device_id=to, device_id_type=MESH)

    low, mid, high = slice(0, R), slice(R, R + T), slice(R + T, W)
    part_rows = R // 4

    def quarter(start, q):
        return pl.ds(pl.multiple_of(start + q * part_rows, part_rows), part_rows)

    pieces = [
        (-1, 0, mask.at[quarter(0, j), :], win.at[quarter(R + T, j), mid]),
        (1, 0, mask.at[quarter(R, j), :], win.at[quarter(0, j), mid]),
        (0, -1, mask.at[:, 0:R], win.at[mid, high]),
        (0, 1, mask.at[:, R:T], win.at[mid, low]),
        (-1, -1, mask.at[0:R, 0:R], win.at[high, high]),
        (-1, 1, mask.at[0:R, R:T], win.at[high, low]),
        (1, -1, mask.at[R:T, 0:R], win.at[low, high]),
        (1, 1, mask.at[R:T, R:T], win.at[low, low]),
    ]
    copies = [remote(src, dst, msend.at[n], mrecv.at[n], device(dr, dc))
              for n, (dr, dc, src, dst) in enumerate(pieces)]
    for n in range(8):
        pl.when(exists(*pieces[n][:2]))(copies[n].start)

    def arrived(n):
        pl.when(exists(-pieces[n][0], -pieces[n][1]))(copies[n].wait_recv)

    def passed(d):
        return [
            remote(win.at[quarter(start, j), mid], win.at[quarter(start, j), mid],
                   psend.at[2 * d - 2 + n], precv.at[2 * d - 2 + n], {"kern": peer[d]})
            for n, start in enumerate((R + T, 0))
        ]

    passes = [passed(d) for d in range(1, 4)]

    for load in loads[1:5] + loads[6:]:
        load.wait()
    sign_row = (1 - 2 * (lax.broadcasted_iota(jnp.int32, (1, R), 1) & 1)).astype(F32)
    sign_col = (1 - 2 * (lax.broadcasted_iota(jnp.int32, (R, 1), 0) & 1)).astype(F32)
    taph[...] = jnp.zeros_like(taph)
    for a in range(PARTS):
        taph[a:a + 1, :] = tapv[a // 3, a % 3, T:T + 1, 0:T]
    edge_h, edge_l = split(taph[...])
    rhat[...] = dot3(edge_h, edge_l, rh[:T, :], rl[:T, :])
    for a in range(PARTS):
        corner = tapv[a // 3, a % 3, T:T + 1, T:T + 1]
        for b in range(2):
            at = slice(b * T + R, b * T + T)
            rhat[a:a + 1, at] = rhat[a:a + 1, at] + corner * sign_row

    def tap_spectrum(a, carry):
        part, k = a // 3, a % 3
        low_h, low_l = split(tapv[part, k, 0:T, 0:T])
        column = tapv[part, k, 0:T, T:T + 1]
        for b in range(2):
            at = slice(b * T, b * T + T)
            value = dot3(low_h, low_l, rh[:T, at], rl[:T, at])
            value = jnp.concatenate([value[:, :R], value[:, R:] + column * sign_row], axis=1)
            vh_, vl_ = split(value)
            xh[:T, at] = vh_
            xl[:T, at] = vl_
        for b in range(2):
            at = slice(b * T, b * T + T)
            value = dot3(th[:, :T], tl[:, :T], xh[:T, at], xl[:T, at])
            edge = sign_col * rhat[a:a + 1, at]
            for f in range(2):
                block = value[f * T:f * T + T]
                block = jnp.concatenate([block[:R], block[R:] + edge], axis=0)
                for n, x in enumerate(to_complex(block)):
                    hs[a, n, f * R:f * R + R, b * R:b * R + R] = x
        return carry

    loop(0, 4, tap_spectrum, 0)

    for n in range(2):
        arrived(n)
        for d in range(3):
            pl.when(exists(-pieces[n][0], 0))(passes[d][n].start)

    loop(4, PARTS, tap_spectrum, 0)

    loads[0].wait()
    for n in range(2, 8):
        arrived(n)
    for d in range(1, 4):
        q = lax.rem(j + 4 - d, 4)
        for n, start in enumerate((R + T, 0)):
            at = win.at[quarter(start, q), mid]
            came = remote(at, at, psend.at[2 * d - 2 + n], precv.at[2 * d - 2 + n], {"kern": peer[d]})
            pl.when(exists(-pieces[n][0], 0))(came.wait_recv)

    for half in range(2):
        up = slice(half * T, half * T + T)
        wh_, wl_ = split(win[up, :])
        for b in range(2):
            at = slice(b * T, b * T + T)
            h_, l_ = split(dot3(wh_, wl_, rh[:, at], rl[:, at]))
            xh[up, at] = h_
            xl[up, at] = l_
    for b in range(2):
        at = slice(b * T, b * T + T)
        value = dot3(th[...], tl[...], xh[:, at], xl[:, at])
        for f in range(2):
            for n, x in enumerate(to_complex(value[f * T:f * T + T])):
                ms[n, f * R:f * R + R, b * R:b * R + R] = x

    def inverse_rows(a, carry):
        for b in range(2):
            for f in range(2):
                at = (slice(f * R, f * R + R), slice(b * R, b * R + R))
                m = [ms[n, at[0], at[1]] for n in range(4)]
                h = [hs[a, n, at[0], at[1]] for n in range(4)]
                y = []
                for n in (0, 2):
                    y.append(m[n] * h[n] + m[n + 1] * h[n + 1])
                    y.append(m[n + 1] * h[n] - m[n] * h[n + 1])
                for n, x in enumerate(from_complex(*y)):
                    h_, l_ = split(x)
                    to = (slice(f * T + (n // 2) * R, f * T + (n // 2) * R + R),
                          slice(b * T + (n % 2) * R, b * T + (n % 2) * R + R))
                    xh[to[0], to[1]] = h_
                    xl[to[0], to[1]] = l_
            at = slice(b * T, b * T + T)
            h_, l_ = split(dot3(rh[:T, :], rl[:T, :], xh[:, at], xl[:, at]))
            vh[a, :, at] = h_
            vl[a, :, at] = l_
        return carry

    loop(0, PARTS, inverse_rows, 0)

    def share_rows(q):
        return pl.ds(pl.multiple_of(q * Q, Q), Q)

    def share_amplitude(d):
        at = share_rows(peer[d])
        value = dot3(vh[:, at, :].reshape(PARTS * Q, W), vl[:, at, :].reshape(PARTS * Q, W),
                     th[:, :T], tl[:, :T]).reshape(PARTS, Q, T) * SCALE
        amp[:, at, :] = value
        total = None
        for k in range(3):
            term = weights[k] * (value[k] * value[k] + value[k + 3] * value[k + 3])
            total = term if total is None else total + term
        return total

    sums = []
    for d in range(1, 4):
        ipart[d - 1] = share_amplitude(d)
        copy = remote(ipart.at[d - 1], irecv.at[d - 1], isend.at[d - 1], isem.at[d - 1], {"kern": peer[d]})
        copy.start()
        sums.append(copy)
    total = share_amplitude(0)
    for copy in sums:
        copy.wait_recv()
    intensity = (total + irecv[0] + irecv[1] + irecv[2]) * (1.0 / 12.0)
    own = share_rows(j)
    resv[own, :] = 1.0 / (1.0 + jnp.exp(-8.0 * (intensity - 0.25)))
    shares = []
    for d in range(1, 4):
        copy = remote(resv.at[own, :], resv.at[own, :], asend.at[d - 1], asem.at[d - 1], {"kern": peer[d]})
        copy.start()
        shares.append(copy)

    loads[5].wait()

    def share_product(q):
        at = share_rows(q)
        x = resv[at, :]
        factor = 2.0 * (x - targ[at, :].astype(F32)) * 8.0 * x * (1.0 - x)
        both = [split(factor * (weights[a % 3] * (2.0 / 12.0)) * amp[a, at, :]) for a in range(PARTS)]
        h_ = jnp.concatenate([x[0] for x in both], axis=0)
        l_ = jnp.concatenate([x[1] for x in both], axis=0)
        for b in range(2):
            cut = slice(b * T, b * T + T)
            u, v = split(dot3(h_, l_, rh[:T, cut], rl[:T, cut]).reshape(PARTS, Q, T))
            ph[:, at, cut] = u
            pw[:, at, cut] = v

    share_product(j)
    for d in range(1, 4):
        q = lax.rem(j + 4 - d, 4)
        rows_q = share_rows(q)
        remote(resv.at[rows_q, :], resv.at[rows_q, :], asend.at[d - 1], asem.at[d - 1],
               {"kern": peer[d]}).wait_recv()
        share_product(q)
    store = pltpu.make_async_copy(resv, resist, lsem.at[7])
    store.start()

    windows = []
    for b in range(2):
        at = slice(b * T, b * T + T)
        acc[...] = jnp.zeros_like(acc)

        def gather(a, carry, at=at, b=b):
            value = dot3(th[:, :T], tl[:, :T], ph[a, :, at], pw[a, :, at])
            for f in range(2):
                p = to_complex(value[f * T:f * T + T])
                fr = slice(f * R, f * R + R)
                h = [hs[a, n, fr, b * R:b * R + R] for n in range(4)]
                for n in (0, 2):
                    acc[n, fr, :] += p[n] * h[n] - p[n + 1] * h[n + 1]
                    acc[n + 1, fr, :] += p[n] * h[n + 1] + p[n + 1] * h[n]
            return carry

        loop(0, PARTS, gather, 0)
        for f in range(2):
            fr = slice(f * R, f * R + R)
            for n, x in enumerate(from_complex(*[acc[i, fr, :] for i in range(4)])):
                h_, l_ = split(x)
                to = (slice(f * T + (n // 2) * R, f * T + (n // 2) * R + R),
                      slice(b * T + (n % 2) * R, b * T + (n % 2) * R + R))
                xh[to[0], to[1]] = h_
                xl[to[0], to[1]] = l_
        tsend[b] = dot3(rh[...], rl[...], xh[:, at], xl[:, at]).reshape(8, Q, T)
        for far in range(2):
            for d in range(1, 4):
                chunk = lax.rem(peer[d] + 6, 8) if far == 0 else peer[d] + 2
                n = (b * 2 + far) * 3 + d - 1
                copy = remote(tsend.at[b, chunk], trecv.at[n], tss.at[n], trs.at[n], {"kern": peer[d]})
                copy.start()
                windows.append(copy)

    for far in range(2):
        for b in range(2):
            n = (b * 2 + far) * 3
            for d in range(3):
                windows[n + d].wait_recv()
            chunk = lax.rem(j + 6, 8) if far == 0 else j + 2
            gw[far * Q:far * Q + Q, b * T:b * T + T] = tsend[b, chunk] + trecv[n] + trecv[n + 1] + trecv[n + 2]
    g_h, g_l = split(gw[...])
    gw[...] = dot3(g_h, g_l, th[...], tl[...])
    far_rows, near_rows = slice(0, Q), slice(Q, 2 * Q)
    west, east = exists(0, -1), exists(0, 1)
    ends = [
        (gives, takes, gw.at[far_rows, mid], ecen, device(step, 0)),
        (jnp.logical_and(gives, west), jnp.logical_and(takes, east), gw.at[far_rows, low], eside.at[0], device(step, -1)),
        (jnp.logical_and(gives, east), jnp.logical_and(takes, west), gw.at[far_rows, high], eside.at[1], device(step, 1)),
        (west, east, gw.at[near_rows, low], eside.at[2], device(0, -1)),
        (east, west, gw.at[near_rows, high], eside.at[3], device(0, 1)),
    ]
    hops = [remote(src, dst, ess.at[n], ers.at[n], to) for n, (_, _, src, dst, to) in enumerate(ends)]
    for n in range(5):
        pl.when(ends[n][0])(hops[n].start)
    lane = lax.broadcasted_iota(jnp.int32, (1, T), 1) // 64
    pixels = jnp.zeros((1, T), F32)
    for k in range(4):
        pixels = jnp.where(lane == k, active[j, k].astype(F32), pixels)
    pixels = pixels * SCALE
    for n in range(5):
        pl.when(ends[n][1])(hops[n].wait_recv)
    own_part = gw[near_rows, mid] + ecen[...]
    outv[:, :R] = (own_part[:, :R] + eside[1] + eside[3]) * pixels[:, :R]
    outv[:, R:] = (own_part[:, R:] + eside[0] + eside[2]) * pixels[:, R:]

    final = pltpu.make_async_copy(outv, gradient, lsem.at[0])
    final.start()

    for n in range(8):
        pl.when(exists(*pieces[n][:2]))(copies[n].wait_send)
    for n in range(2):
        for d in range(3):
            pl.when(exists(-pieces[n][0], 0))(passes[d][n].wait_send)
    for copy in sums + shares + windows:
        copy.wait_send()
    for n in range(5):
        pl.when(ends[n][0])(hops[n].wait_send)
    store.wait()
    final.wait()


def local(photomask, target_bits, active_blocks, kernel_taps, kernel_weights):
    hbm = pl.BlockSpec(memory_space=pl.ANY)
    smem = pl.BlockSpec(memory_space=pltpu.SMEM)
    vmem = pltpu.VMEM
    dma = pltpu.SemaphoreType.DMA
    scratch = [
        vmem((W, W), F32),
        vmem((2, 3, 2 * R + 1, 2 * R + 1), F32),
        vmem((W, W), BF), vmem((W, W), BF), vmem((W, W), BF), vmem((W, W), BF),
        vmem((T, T), jnp.int32),
        vmem((8, T), F32),
        vmem((8, W), F32),
        vmem((W, W), BF), vmem((W, W), BF),
        vmem((PARTS, 4, T, T), F32),
        vmem((4, T, T), F32),
        vmem((PARTS, T, W), BF), vmem((PARTS, T, W), BF),
        vmem((PARTS, T, T), F32),
        vmem((PARTS, T, W), BF), vmem((PARTS, T, W), BF),
        vmem((3, Q, T), F32), vmem((3, Q, T), F32),
        vmem((T, T), F32),
        vmem((4, T, R), F32),
        vmem((2, 8, Q, T), F32),
        vmem((12, Q, T), F32),
        vmem((2 * Q, W), F32),
        vmem((Q, T), F32), vmem((4, Q, R), F32),
        vmem((Q, T), F32),
        dma((14,)), dma((8,)), dma((8,)),
        dma((6,)), dma((6,)),
        dma((3,)), dma((3,)), dma((3,)), dma((3,)),
        dma((12,)), dma((12,)),
        dma((5,)), dma((5,)),
    ]
    outs = (jax.ShapeDtypeStruct((Q, T), F32), jax.ShapeDtypeStruct((T, T), F32))
    gradient, resist = pl.pallas_call(
        kernel,
        out_shape=outs,
        in_specs=[hbm, hbm, smem, hbm, smem, hbm, hbm, hbm, hbm],
        out_specs=(hbm, hbm),
        scratch_shapes=scratch,
        compiler_params=pltpu.CompilerParams(
            collective_id=0, has_side_effects=True, vmem_limit_bytes=56 * 1024 * 1024),
        name="socs",
    )(photomask, target_bits, active_blocks, kernel_taps.transpose(1, 2, 0, 3), kernel_weights,
      *[jnp.asarray(t) for t in tables()])
    return pl.pallas_call(hand_over, out_shape=outs, name="hand_over")(gradient, resist)


def solution(mesh):
    in_specs = (
        P("row", "col"),
        P("row", "col"),
        P("row", "col"),
        P(None, "kern", None, None),
        P("kern"),
    )
    out_specs = (P(("row", "kern"), "col"), P("row", "col"))
    return jax.shard_map(local, mesh=mesh, in_specs=in_specs, out_specs=out_specs, check_vma=False)
```

```python
import functools

import jax
import jax.numpy as jnp
import numpy as np
from jax import lax
from jax.experimental import pallas as pl
from jax.experimental.pallas import tpu as pltpu
from jax.sharding import PartitionSpec as P

MESH = pl.DeviceIdType.MESH
T = 256
W = 512
R = 128
PARTS = 6
Q = 64
SCALE = 2.0 ** -17
F32 = jnp.float32
BF = jnp.bfloat16


def tables():
    sample = np.arange(W)[:, None]
    freq = np.arange(T)[None, :]
    angle = np.pi / W * (sample * (2 * freq + 1) % (2 * W))
    cos, sin = np.cos(angle), np.sin(angle)
    full = np.concatenate([cos[:, :R], sin[:, :R], cos[:, R:], sin[:, R:]], axis=1)
    full[np.abs(full) < 1e-12] = 0.0
    high = full.astype(BF)
    low = (full - high.astype(np.float64)).astype(BF)
    return high, low, np.ascontiguousarray(high.T), np.ascontiguousarray(low.T)


def split(value):
    high = value.astype(BF)
    return high, (value - high.astype(F32)).astype(BF)


def dot(a, b):
    return jnp.dot(a, b, preferred_element_type=F32)


def dot3(ah, al, bh, bl):
    return dot(ah, bh) + dot(al, bh) + dot(ah, bl)


def to_complex(block):
    cc, cs = block[:R, :R], block[:R, R:]
    sc, ss = block[R:, :R], block[R:, R:]
    return cc - ss, -(cs + sc), cc + ss, cs - sc


def from_complex(pr, pi, mr, mi):
    return pr + mr, mi - pi, -(pi + mi), mr - pr


def hand_over(gradient, resist, gradient_out, resist_out, sems):
    copies = [
        pltpu.make_async_copy(resist, resist_out, sems.at[0]),
        pltpu.make_async_copy(gradient, gradient_out, sems.at[1]),
    ]
    for copy in copies:
        copy.start()
    for copy in copies:
        copy.wait()


def loop(lo, hi, fn, init):
    for i in range(lo, hi):
        fn(i, init)


def kernel(
    mask, target, active, taps, weights, rh_in, rl_in, th_in, tl_in,
    gradient, resist,
    win, tapv, rh, rl, th, tl, targ, taph, rhat, xh, xl, mpart, hs, ms, vh, vl, amp, ph, pw,
    ipart, ione, imid, itwo, resv, acc, tsend, tone, tmid, ttwo, gw, ecen, eside, outv,
    lsem, msend, mrecv, psend, precv, isend, isem, asend, asem, tss, trs, uss, urs, ess, ers,
):
    r, c, j = lax.axis_index("row"), lax.axis_index("col"), lax.axis_index("kern")
    rows, cols = lax.axis_size("row"), lax.axis_size("col")
    def exists(dr, dc):
        ok = None
        for at, d, n in ((r, dr, rows), (c, dc, cols)):
            if d:
                one = at > 0 if d < 0 else at < n - 1
                ok = one if ok is None else jnp.logical_and(ok, one)
        return ok

    def device(dr, dc):
        return {"row": r + dr, "col": c + dc}

    around = [(dr, dc) for dr in (-1, 0, 1) for dc in (-1, 0, 1) if dr or dc]
    down = j < 2
    step = jnp.where(down, 1, -1)
    gives = jnp.logical_or(jnp.logical_and(down, r < rows - 1), jnp.logical_and(jnp.logical_not(down), r > 0))
    takes = jnp.logical_or(jnp.logical_and(down, r > 0), jnp.logical_and(jnp.logical_not(down), r < rows - 1))
    peer = [lax.rem(j + d, 4) for d in range(4)]

    ecen[...] = jnp.zeros_like(ecen)
    eside[...] = jnp.zeros_like(eside)
    barrier = pltpu.get_barrier_semaphore()
    count = 3
    for dr, dc in around:
        ok = exists(dr, dc)
        count = count + ok.astype(jnp.int32)

        @pl.when(ok)
        def _(dr=dr, dc=dc):
            pl.semaphore_signal(barrier, inc=1, device_id=device(dr, dc), device_id_type=MESH)
    for d in range(1, 4):
        pl.semaphore_signal(barrier, inc=1, device_id={"kern": peer[d]}, device_id_type=MESH)
    loads = [
        pltpu.make_async_copy(mask, win.at[R:R + T, R:R + T], lsem.at[0]),
        pltpu.make_async_copy(rh_in, rh, lsem.at[1]),
        pltpu.make_async_copy(rl_in, rl, lsem.at[2]),
        pltpu.make_async_copy(th_in, th, lsem.at[3]),
        pltpu.make_async_copy(tl_in, tl, lsem.at[4]),
        pltpu.make_async_copy(target, targ, lsem.at[5]),
    ]
    loads += [
        pltpu.make_async_copy(taps.at[a % 3, :, a // 3, :], tapv.at[a // 3, a % 3], lsem.at[8 + a])
        for a in range(PARTS)
    ]
    for load in loads:
        load.start()

    @pl.when(r == 0)
    def _():
        win[:R, :] = jnp.zeros((R, W), F32)

    @pl.when(r == rows - 1)
    def _():
        win[R + T:, :] = jnp.zeros((R, W), F32)

    @pl.when(c == 0)
    def _():
        win[:, :R] = jnp.zeros((W, R), F32)

    @pl.when(c == cols - 1)
    def _():
        win[:, R + T:] = jnp.zeros((W, R), F32)

    pl.semaphore_wait(barrier, count)

    def remote(src, dst, s, d, to):
        return pltpu.make_async_remote_copy(
            src_ref=src, dst_ref=dst, send_sem=s, recv_sem=d, device_id=to, device_id_type=MESH)

    low, mid, high = slice(0, R), slice(R, R + T), slice(R + T, W)
    part_rows = R // 4

    def quarter(start, q):
        return pl.ds(pl.multiple_of(start + q * part_rows, part_rows), part_rows)

    pieces = [
        (-1, 0, mask.at[quarter(0, j), :], win.at[quarter(R + T, j), mid]),
        (1, 0, mask.at[quarter(R, j), :], win.at[quarter(0, j), mid]),
        (0, -1, mask.at[:, 0:R], win.at[mid, high]),
        (0, 1, mask.at[:, R:T], win.at[mid, low]),
        (-1, -1, mask.at[0:R, 0:R], win.at[high, high]),
        (-1, 1, mask.at[0:R, R:T], win.at[high, low]),
        (1, -1, mask.at[R:T, 0:R], win.at[low, high]),
        (1, 1, mask.at[R:T, R:T], win.at[low, low]),
    ]
    copies = [remote(src, dst, msend.at[n], mrecv.at[n], device(dr, dc))
              for n, (dr, dc, src, dst) in enumerate(pieces)]
    for n in range(8):
        pl.when(exists(*pieces[n][:2]))(copies[n].start)

    def arrived(n):
        pl.when(exists(-pieces[n][0], -pieces[n][1]))(copies[n].wait_recv)

    def passed(d):
        return [
            remote(win.at[quarter(start, j), mid], win.at[quarter(start, j), mid],
                   psend.at[2 * d - 2 + n], precv.at[2 * d - 2 + n], {"kern": peer[d]})
            for n, start in enumerate((R + T, 0))
        ]

    passes = [passed(d) for d in range(1, 4)]

    for load in loads[1:5] + loads[6:]:
        load.wait()
    sign_row = (1 - 2 * (lax.broadcasted_iota(jnp.int32, (1, R), 1) & 1)).astype(F32)
    sign_col = (1 - 2 * (lax.broadcasted_iota(jnp.int32, (R, 1), 0) & 1)).astype(F32)
    taph[...] = jnp.zeros_like(taph)
    for a in range(PARTS):
        taph[a:a + 1, :] = tapv[a // 3, a % 3, T:T + 1, 0:T]
    edge_h, edge_l = split(taph[...])
    rhat[...] = dot3(edge_h, edge_l, rh[:T, :], rl[:T, :])
    for a in range(PARTS):
        corner = tapv[a // 3, a % 3, T:T + 1, T:T + 1]
        for b in range(2):
            at = slice(b * T + R, b * T + T)
            rhat[a:a + 1, at] = rhat[a:a + 1, at] + corner * sign_row

    def tap_spectrum(a, carry):
        part, k = a // 3, a % 3
        low_h, low_l = split(tapv[part, k, 0:T, 0:T])
        column = tapv[part, k, 0:T, T:T + 1]
        for b in range(2):
            at = slice(b * T, b * T + T)
            value = dot3(low_h, low_l, rh[:T, at], rl[:T, at])
            value = jnp.concatenate([value[:, :R], value[:, R:] + column * sign_row], axis=1)
            vh_, vl_ = split(value)
            xh[:T, at] = vh_
            xl[:T, at] = vl_
        for b in range(2):
            at = slice(b * T, b * T + T)
            value = dot3(th[:, :T], tl[:, :T], xh[:T, at], xl[:T, at])
            edge = sign_col * rhat[a:a + 1, at]
            for f in range(2):
                block = value[f * T:f * T + T]
                block = jnp.concatenate([block[:R], block[R:] + edge], axis=0)
                for n, x in enumerate(to_complex(block)):
                    hs[a, n, f * R:f * R + R, b * R:b * R + R] = x
        return carry

    loop(0, 4, tap_spectrum, 0)

    for n in range(2):
        arrived(n)
        for d in range(3):
            pl.when(exists(-pieces[n][0], 0))(passes[d][n].start)

    loop(4, PARTS, tap_spectrum, 0)

    loads[0].wait()
    for n in (2, 3):
        arrived(n)

    def mask_columns(values):
        h_, l_ = split(values)
        return [split(dot3(h_, l_, rh[:, b * T:b * T + T], rl[:, b * T:b * T + T])) for b in range(2)]

    for b, (h_, l_) in enumerate(mask_columns(win[mid, :])):
        mpart[:, b * T:b * T + T] = dot3(th[:, mid], tl[:, mid], h_, l_)

    for n in range(4, 8):
        arrived(n)
    for d in range(1, 4):
        q = lax.rem(j + 4 - d, 4)
        for n, start in enumerate((R + T, 0)):
            at = win.at[quarter(start, q), mid]
            came = remote(at, at, psend.at[2 * d - 2 + n], precv.at[2 * d - 2 + n], {"kern": peer[d]})
            pl.when(exists(-pieces[n][0], 0))(came.wait_recv)

    outer = [jnp.concatenate([t[:, low], t[:, high]], axis=1) for t in (th, tl)]
    for b, (h_, l_) in enumerate(mask_columns(jnp.concatenate([win[low, :], win[high, :]], axis=0))):
        value = mpart[:, b * T:b * T + T] + dot3(*outer, h_, l_)
        for f in range(2):
            for n, x in enumerate(to_complex(value[f * T:f * T + T])):
                ms[n, f * R:f * R + R, b * R:b * R + R] = x

    def inverse_rows(a, carry):
        for b in range(2):
            for f in range(2):
                at = (slice(f * R, f * R + R), slice(b * R, b * R + R))
                m = [ms[n, at[0], at[1]] for n in range(4)]
                h = [hs[a, n, at[0], at[1]] for n in range(4)]
                y = []
                for n in (0, 2):
                    y.append(m[n] * h[n] + m[n + 1] * h[n + 1])
                    y.append(m[n + 1] * h[n] - m[n] * h[n + 1])
                for n, x in enumerate(from_complex(*y)):
                    h_, l_ = split(x)
                    to = (slice(f * T + (n // 2) * R, f * T + (n // 2) * R + R),
                          slice(b * T + (n % 2) * R, b * T + (n % 2) * R + R))
                    xh[to[0], to[1]] = h_
                    xl[to[0], to[1]] = l_
            at = slice(b * T, b * T + T)
            h_, l_ = split(dot3(rh[:T, :], rl[:T, :], xh[:, at], xl[:, at]))
            vh[a, :, at] = h_
            vl[a, :, at] = l_
        return carry

    loop(0, PARTS, inverse_rows, 0)

    def partner(kind, at):
        return at + 1 - 2 * lax.rem(at, 2) if kind == 0 else 3 - at

    pair = (partner(0, j), partner(1, j))
    def rows_of(i):
        return slice(i * Q, i * Q + Q)

    def amplitudes(i):
        at = rows_of(i)
        value = dot3(vh[:, at, :].reshape(PARTS * Q, W), vl[:, at, :].reshape(PARTS * Q, W),
                     th[:, :T], tl[:, :T]).reshape(PARTS, Q, T) * SCALE
        amp[:, at, :] = value
        total = None
        for k in range(3):
            term = weights[k] * (value[k] * value[k] + value[k + 3] * value[k + 3])
            total = term if total is None else total + term
        return total

    halves = (slice(0, R), slice(R, T))
    sums = []
    for i in range(4):
        ipart[i] = amplitudes(i)
        for half in range(2):
            n = 2 * i + half
            copy = remote(ipart.at[i, :, halves[half]], ione.at[n], isend.at[n], isem.at[n], {"kern": pair[half]})
            copy.start()
            sums.append(copy)
    shares = []
    for i in range(4):
        for half in range(2):
            n = 2 * i + half
            sums[n].wait_recv()
            imid[n] = ipart[i, :, halves[half]] + ione[n]
            copy = remote(imid.at[n], itwo.at[n], asend.at[n], asem.at[n], {"kern": pair[1 - half]})
            copy.start()
            shares.append(copy)

    loads[5].wait()
    for i in range(4):
        at = rows_of(i)
        for half in range(2):
            shares[2 * i + half].wait_recv()
        intensity = jnp.concatenate([imid[2 * i] + itwo[2 * i], imid[2 * i + 1] + itwo[2 * i + 1]], axis=1) * (1.0 / 12.0)
        x = 1.0 / (1.0 + jnp.exp(-8.0 * (intensity - 0.25)))
        resv[at, :] = x
        factor = 2.0 * (x - targ[at, :].astype(F32)) * 8.0 * x * (1.0 - x)
        both = [split(factor * (weights[a % 3] * (2.0 / 12.0)) * amp[a, at, :]) for a in range(PARTS)]
        h_ = jnp.concatenate([x[0] for x in both], axis=0)
        l_ = jnp.concatenate([x[1] for x in both], axis=0)
        for b in range(2):
            cut = slice(b * T, b * T + T)
            u, v = split(dot3(h_, l_, rh[:T, cut], rl[:T, cut]).reshape(PARTS, Q, T))
            ph[:, at, cut] = u
            pw[:, at, cut] = v
    store = pltpu.make_async_copy(resv, resist, lsem.at[7])
    store.start()

    firsts = []
    for b in range(2):
        at = slice(b * T, b * T + T)
        acc[...] = jnp.zeros_like(acc)

        def gather(a, carry, at=at, b=b):
            value = dot3(th[:, :T], tl[:, :T], ph[a, :, at], pw[a, :, at])
            for f in range(2):
                p = to_complex(value[f * T:f * T + T])
                fr = slice(f * R, f * R + R)
                h = [hs[a, n, fr, b * R:b * R + R] for n in range(4)]
                for n in (0, 2):
                    acc[n, fr, :] += p[n] * h[n] - p[n + 1] * h[n + 1]
                    acc[n + 1, fr, :] += p[n] * h[n + 1] + p[n + 1] * h[n]
            return carry

        loop(0, PARTS, gather, 0)
        for f in range(2):
            fr = slice(f * R, f * R + R)
            for n, x in enumerate(from_complex(*[acc[i, fr, :] for i in range(4)])):
                h_, l_ = split(x)
                to = (slice(f * T + (n // 2) * R, f * T + (n // 2) * R + R),
                      slice(b * T + (n % 2) * R, b * T + (n % 2) * R + R))
                xh[to[0], to[1]] = h_
                xl[to[0], to[1]] = l_
        value = dot3(rh[...], rl[...], xh[:, at], xl[:, at])
        for q in range(4):
            for far in range(2):
                m = (q + 6) % 8 if far == 0 else q + 2
                tsend[b, q, far] = value[m * Q:m * Q + Q]
        for half in range(2):
            to = pair[half]
            for slot, owner in enumerate((to, partner(1 - half, to))):
                n = (b * 2 + half) * 2 + slot
                copy = remote(tsend.at[b, owner, :, :, half * R:half * R + R], tone.at[n],
                              tss.at[n], trs.at[n], {"kern": to})
                copy.start()
                firsts.append(copy)

    seconds = []
    for b in range(2):
        for half in range(2):
            n = b * 2 + half
            firsts[2 * n].wait_recv()
            firsts[2 * n + 1].wait_recv()
            to = pair[1 - half]
            tmid[n] = tsend[b, to, :, :, half * R:half * R + R] + tone[2 * n + 1]
            copy = remote(tmid.at[n], ttwo.at[n], uss.at[n], urs.at[n], {"kern": to})
            copy.start()
            seconds.append(copy)

    for b in range(2):
        for half in range(2):
            n = b * 2 + half
            seconds[n].wait_recv()
            part = tsend[b, j, :, :, half * R:half * R + R] + tone[2 * n] + ttwo[n]
            gw[:, b * T + half * R:b * T + half * R + R] = part.reshape(2 * Q, R)
    g_h, g_l = split(gw[...])
    gw[...] = dot3(g_h, g_l, th[...], tl[...])
    far_rows, near_rows = slice(0, Q), slice(Q, 2 * Q)
    west, east = exists(0, -1), exists(0, 1)
    ends = [
        (gives, takes, gw.at[far_rows, mid], ecen, device(step, 0)),
        (jnp.logical_and(gives, west), jnp.logical_and(takes, east), gw.at[far_rows, low], eside.at[0], device(step, -1)),
        (jnp.logical_and(gives, east), jnp.logical_and(takes, west), gw.at[far_rows, high], eside.at[1], device(step, 1)),
        (west, east, gw.at[near_rows, low], eside.at[2], device(0, -1)),
        (east, west, gw.at[near_rows, high], eside.at[3], device(0, 1)),
    ]
    hops = [remote(src, dst, ess.at[n], ers.at[n], to) for n, (_, _, src, dst, to) in enumerate(ends)]
    for n in range(5):
        pl.when(ends[n][0])(hops[n].start)
    lane = lax.broadcasted_iota(jnp.int32, (1, T), 1) // 64
    pixels = jnp.zeros((1, T), F32)
    for k in range(4):
        pixels = jnp.where(lane == k, active[j, k].astype(F32), pixels)
    pixels = pixels * SCALE
    for n in range(5):
        pl.when(ends[n][1])(hops[n].wait_recv)
    own_part = gw[near_rows, mid] + ecen[...]
    outv[:, :R] = (own_part[:, :R] + eside[1] + eside[3]) * pixels[:, :R]
    outv[:, R:] = (own_part[:, R:] + eside[0] + eside[2]) * pixels[:, R:]

    final = pltpu.make_async_copy(outv, gradient, lsem.at[0])
    final.start()

    for n in range(8):
        pl.when(exists(*pieces[n][:2]))(copies[n].wait_send)
    for n in range(2):
        for d in range(3):
            pl.when(exists(-pieces[n][0], 0))(passes[d][n].wait_send)
    for copy in sums + shares + firsts + seconds:
        copy.wait_send()
    for n in range(5):
        pl.when(ends[n][0])(hops[n].wait_send)
    store.wait()
    final.wait()


def local(photomask, target_bits, active_blocks, kernel_taps, kernel_weights):
    hbm = pl.BlockSpec(memory_space=pl.ANY)
    smem = pl.BlockSpec(memory_space=pltpu.SMEM)
    vmem = pltpu.VMEM
    dma = pltpu.SemaphoreType.DMA
    scratch = [
        vmem((W, W), F32),
        vmem((2, 3, 2 * R + 1, 2 * R + 1), F32),
        vmem((W, W), BF), vmem((W, W), BF), vmem((W, W), BF), vmem((W, W), BF),
        vmem((T, T), jnp.int32),
        vmem((8, T), F32),
        vmem((8, W), F32),
        vmem((W, W), BF), vmem((W, W), BF),
        vmem((W, W), F32),
        vmem((PARTS, 4, T, T), F32),
        vmem((4, T, T), F32),
        vmem((PARTS, T, W), BF), vmem((PARTS, T, W), BF),
        vmem((PARTS, T, T), F32),
        vmem((PARTS, T, W), BF), vmem((PARTS, T, W), BF),
        vmem((4, Q, T), F32), vmem((8, Q, R), F32), vmem((8, Q, R), F32), vmem((8, Q, R), F32),
        vmem((T, T), F32),
        vmem((4, T, R), F32),
        vmem((2, 4, 2, Q, T), F32),
        vmem((8, 2, Q, R), F32), vmem((4, 2, Q, R), F32), vmem((4, 2, Q, R), F32),
        vmem((2 * Q, W), F32),
        vmem((Q, T), F32), vmem((4, Q, R), F32),
        vmem((Q, T), F32),
        dma((14,)), dma((8,)), dma((8,)),
        dma((6,)), dma((6,)),
        dma((8,)), dma((8,)), dma((8,)), dma((8,)),
        dma((8,)), dma((8,)), dma((4,)), dma((4,)),
        dma((5,)), dma((5,)),
    ]
    outs = (jax.ShapeDtypeStruct((Q, T), F32), jax.ShapeDtypeStruct((T, T), F32))
    gradient, resist = pl.pallas_call(
        kernel,
        out_shape=outs,
        in_specs=[hbm, hbm, smem, hbm, smem, hbm, hbm, hbm, hbm],
        out_specs=(hbm, hbm),
        scratch_shapes=scratch,
        compiler_params=pltpu.CompilerParams(
            collective_id=0, has_side_effects=True, vmem_limit_bytes=56 * 1024 * 1024),
        name="socs",
    )(photomask, target_bits, active_blocks, kernel_taps.transpose(1, 2, 0, 3), kernel_weights,
      *[jnp.asarray(t) for t in tables()])
    return pl.pallas_call(
        hand_over, out_shape=outs, in_specs=[hbm, hbm], out_specs=(hbm, hbm), scratch_shapes=[dma((2,))],
        name="hand_over")(gradient, resist)


def solution(mesh):
    in_specs = (
        P("row", "col"),
        P("row", "col"),
        P("row", "col"),
        P(None, "kern", None, None),
        P("kern"),
    )
    out_specs = (P(("row", "kern"), "col"), P("row", "col"))
    return jax.shard_map(local, mesh=mesh, in_specs=in_specs, out_specs=out_specs, check_vma=False)
```

```python
import functools

import jax
import jax.numpy as jnp
import numpy as np
from jax import lax
from jax.experimental import pallas as pl
from jax.experimental.pallas import tpu as pltpu
from jax.sharding import PartitionSpec as P

MESH = pl.DeviceIdType.MESH
T = 256
W = 512
R = 128
PARTS = 6
Q = 64
SCALE = 2.0 ** -17
F32 = jnp.float32
BF = jnp.bfloat16


def tables():
    sample = np.arange(W)[:, None]
    freq = np.arange(T)[None, :]
    angle = np.pi / W * (sample * (2 * freq + 1) % (2 * W))
    cos, sin = np.cos(angle), np.sin(angle)
    full = np.concatenate([cos[:, :R], sin[:, :R], cos[:, R:], sin[:, R:]], axis=1)
    full[np.abs(full) < 1e-12] = 0.0
    high = full.astype(BF)
    low = (full - high.astype(np.float64)).astype(BF)
    return high, low, np.ascontiguousarray(high.T), np.ascontiguousarray(low.T)


def split(value):
    high = value.astype(BF)
    return high, (value - high.astype(F32)).astype(BF)


def dot(a, b):
    return jnp.dot(a, b, preferred_element_type=F32)


def dot3(ah, al, bh, bl):
    return dot(ah, bh) + dot(al, bh) + dot(ah, bl)


def to_complex(block):
    cc, cs = block[:R, :R], block[:R, R:]
    sc, ss = block[R:, :R], block[R:, R:]
    return cc - ss, -(cs + sc), cc + ss, cs - sc


def from_complex(pr, pi, mr, mi):
    return pr + mr, mi - pi, -(pi + mi), mr - pr


def hand_over(gradient, resist, gradient_out, resist_out):
    gradient_out[...] = gradient[...]
    resist_out[...] = resist[...]


def loop(lo, hi, fn, init):
    for i in range(lo, hi):
        fn(i, init)


def kernel(
    mask, target, active, taps, weights, rh_in, rl_in, th_in, tl_in,
    gradient, resist,
    win, tapv, rh, rl, th, tl, targ, taph, rhat, xh, xl, mpart, hs, ms, vh, vl, amp, ph, pw,
    ipart, ione, imid, itwo, resv, acc, tsend, tone, tmid, ttwo, gw, ecen, eside, outv,
    lsem, msend, mrecv, psend, precv, isend, isem, asend, asem, tss, trs, uss, urs, ess, ers,
):
    r, c, j = lax.axis_index("row"), lax.axis_index("col"), lax.axis_index("kern")
    rows, cols = lax.axis_size("row"), lax.axis_size("col")
    def exists(dr, dc):
        ok = None
        for at, d, n in ((r, dr, rows), (c, dc, cols)):
            if d:
                one = at > 0 if d < 0 else at < n - 1
                ok = one if ok is None else jnp.logical_and(ok, one)
        return ok

    def device(dr, dc):
        return {"row": r + dr, "col": c + dc}

    around = [(dr, dc) for dr in (-1, 0, 1) for dc in (-1, 0, 1) if dr or dc]
    down = j < 2
    step = jnp.where(down, 1, -1)
    gives = jnp.logical_or(jnp.logical_and(down, r < rows - 1), jnp.logical_and(jnp.logical_not(down), r > 0))
    takes = jnp.logical_or(jnp.logical_and(down, r > 0), jnp.logical_and(jnp.logical_not(down), r < rows - 1))
    peer = [lax.rem(j + d, 4) for d in range(4)]

    ecen[...] = jnp.zeros_like(ecen)
    eside[...] = jnp.zeros_like(eside)
    barrier = pltpu.get_barrier_semaphore()
    count = 3
    for dr, dc in around:
        ok = exists(dr, dc)
        count = count + ok.astype(jnp.int32)

        @pl.when(ok)
        def _(dr=dr, dc=dc):
            pl.semaphore_signal(barrier, inc=1, device_id=device(dr, dc), device_id_type=MESH)
    for d in range(1, 4):
        pl.semaphore_signal(barrier, inc=1, device_id={"kern": peer[d]}, device_id_type=MESH)
    loads = [
        pltpu.make_async_copy(mask, win.at[R:R + T, R:R + T], lsem.at[0]),
        pltpu.make_async_copy(rh_in, rh, lsem.at[1]),
        pltpu.make_async_copy(rl_in, rl, lsem.at[2]),
        pltpu.make_async_copy(th_in, th, lsem.at[3]),
        pltpu.make_async_copy(tl_in, tl, lsem.at[4]),
        pltpu.make_async_copy(target, targ, lsem.at[5]),
    ]
    loads += [
        pltpu.make_async_copy(taps.at[a % 3, :, a // 3, :], tapv.at[a // 3, a % 3], lsem.at[8 + a])
        for a in range(PARTS)
    ]
    for load in loads:
        load.start()

    @pl.when(r == 0)
    def _():
        win[:R, :] = jnp.zeros((R, W), F32)

    @pl.when(r == rows - 1)
    def _():
        win[R + T:, :] = jnp.zeros((R, W), F32)

    @pl.when(c == 0)
    def _():
        win[:, :R] = jnp.zeros((W, R), F32)

    @pl.when(c == cols - 1)
    def _():
        win[:, R + T:] = jnp.zeros((W, R), F32)

    pl.semaphore_wait(barrier, count)

    def remote(src, dst, s, d, to):
        return pltpu.make_async_remote_copy(
            src_ref=src, dst_ref=dst, send_sem=s, recv_sem=d, device_id=to, device_id_type=MESH)

    low, mid, high = slice(0, R), slice(R, R + T), slice(R + T, W)
    part_rows = R // 4

    def quarter(start, q):
        return pl.ds(pl.multiple_of(start + q * part_rows, part_rows), part_rows)

    pieces = [
        (-1, 0, mask.at[quarter(0, j), :], win.at[quarter(R + T, j), mid]),
        (1, 0, mask.at[quarter(R, j), :], win.at[quarter(0, j), mid]),
        (0, -1, mask.at[:, 0:R], win.at[mid, high]),
        (0, 1, mask.at[:, R:T], win.at[mid, low]),
        (-1, -1, mask.at[0:R, 0:R], win.at[high, high]),
        (-1, 1, mask.at[0:R, R:T], win.at[high, low]),
        (1, -1, mask.at[R:T, 0:R], win.at[low, high]),
        (1, 1, mask.at[R:T, R:T], win.at[low, low]),
    ]
    copies = [remote(src, dst, msend.at[n], mrecv.at[n], device(dr, dc))
              for n, (dr, dc, src, dst) in enumerate(pieces)]
    for n in range(8):
        pl.when(exists(*pieces[n][:2]))(copies[n].start)

    def arrived(n):
        pl.when(exists(-pieces[n][0], -pieces[n][1]))(copies[n].wait_recv)

    def passed(d):
        return [
            remote(win.at[quarter(start, j), mid], win.at[quarter(start, j), mid],
                   psend.at[2 * d - 2 + n], precv.at[2 * d - 2 + n], {"kern": peer[d]})
            for n, start in enumerate((R + T, 0))
        ]

    passes = [passed(d) for d in range(1, 4)]

    for load in loads[1:5] + loads[6:]:
        load.wait()
    sign_row = (1 - 2 * (lax.broadcasted_iota(jnp.int32, (1, R), 1) & 1)).astype(F32)
    sign_col = (1 - 2 * (lax.broadcasted_iota(jnp.int32, (R, 1), 0) & 1)).astype(F32)
    taph[...] = jnp.zeros_like(taph)
    for a in range(PARTS):
        taph[a:a + 1, :] = tapv[a // 3, a % 3, T:T + 1, 0:T]
    edge_h, edge_l = split(taph[...])
    rhat[...] = dot3(edge_h, edge_l, rh[:T, :], rl[:T, :])
    for a in range(PARTS):
        corner = tapv[a // 3, a % 3, T:T + 1, T:T + 1]
        for b in range(2):
            at = slice(b * T + R, b * T + T)
            rhat[a:a + 1, at] = rhat[a:a + 1, at] + corner * sign_row

    def tap_spectrum(a, carry):
        part, k = a // 3, a % 3
        low_h, low_l = split(tapv[part, k, 0:T, 0:T])
        column = tapv[part, k, 0:T, T:T + 1]
        for b in range(2):
            at = slice(b * T, b * T + T)
            value = dot3(low_h, low_l, rh[:T, at], rl[:T, at])
            value = jnp.concatenate([value[:, :R], value[:, R:] + column * sign_row], axis=1)
            vh_, vl_ = split(value)
            xh[:T, at] = vh_
            xl[:T, at] = vl_
        for b in range(2):
            at = slice(b * T, b * T + T)
            value = dot3(th[:, :T], tl[:, :T], xh[:T, at], xl[:T, at])
            edge = sign_col * rhat[a:a + 1, at]
            for f in range(2):
                block = value[f * T:f * T + T]
                block = jnp.concatenate([block[:R], block[R:] + edge], axis=0)
                for n, x in enumerate(to_complex(block)):
                    hs[a, n, f * R:f * R + R, b * R:b * R + R] = x
        return carry

    loop(0, 4, tap_spectrum, 0)

    for n in range(2):
        arrived(n)
        for d in range(3):
            pl.when(exists(-pieces[n][0], 0))(passes[d][n].start)

    loop(4, PARTS, tap_spectrum, 0)

    loads[0].wait()
    for n in (2, 3):
        arrived(n)

    def mask_columns(values):
        h_, l_ = split(values)
        return [split(dot3(h_, l_, rh[:, b * T:b * T + T], rl[:, b * T:b * T + T])) for b in range(2)]

    for b, (h_, l_) in enumerate(mask_columns(win[mid, :])):
        mpart[:, b * T:b * T + T] = dot3(th[:, mid], tl[:, mid], h_, l_)

    for n in range(4, 8):
        arrived(n)
    for d in range(1, 4):
        q = lax.rem(j + 4 - d, 4)
        for n, start in enumerate((R + T, 0)):
            at = win.at[quarter(start, q), mid]
            came = remote(at, at, psend.at[2 * d - 2 + n], precv.at[2 * d - 2 + n], {"kern": peer[d]})
            pl.when(exists(-pieces[n][0], 0))(came.wait_recv)

    outer = [jnp.concatenate([t[:, low], t[:, high]], axis=1) for t in (th, tl)]
    for b, (h_, l_) in enumerate(mask_columns(jnp.concatenate([win[low, :], win[high, :]], axis=0))):
        value = mpart[:, b * T:b * T + T] + dot3(*outer, h_, l_)
        for f in range(2):
            for n, x in enumerate(to_complex(value[f * T:f * T + T])):
                ms[n, f * R:f * R + R, b * R:b * R + R] = x

    def inverse_rows(a, carry):
        for b in range(2):
            for f in range(2):
                at = (slice(f * R, f * R + R), slice(b * R, b * R + R))
                m = [ms[n, at[0], at[1]] for n in range(4)]
                h = [hs[a, n, at[0], at[1]] for n in range(4)]
                y = []
                for n in (0, 2):
                    y.append(m[n] * h[n] + m[n + 1] * h[n + 1])
                    y.append(m[n + 1] * h[n] - m[n] * h[n + 1])
                for n, x in enumerate(from_complex(*y)):
                    h_, l_ = split(x)
                    to = (slice(f * T + (n // 2) * R, f * T + (n // 2) * R + R),
                          slice(b * T + (n % 2) * R, b * T + (n % 2) * R + R))
                    xh[to[0], to[1]] = h_
                    xl[to[0], to[1]] = l_
            at = slice(b * T, b * T + T)
            h_, l_ = split(dot3(rh[:T, :], rl[:T, :], xh[:, at], xl[:, at]))
            vh[a, :, at] = h_
            vl[a, :, at] = l_
        return carry

    loop(0, PARTS, inverse_rows, 0)

    def partner(kind, at):
        return at + 1 - 2 * lax.rem(at, 2) if kind == 0 else 3 - at

    pair = (partner(0, j), partner(1, j))
    def rows_of(i):
        return slice(i * Q, i * Q + Q)

    def amplitudes(i):
        at = rows_of(i)
        value = dot3(vh[:, at, :].reshape(PARTS * Q, W), vl[:, at, :].reshape(PARTS * Q, W),
                     th[:, :T], tl[:, :T]).reshape(PARTS, Q, T) * SCALE
        amp[:, at, :] = value
        total = None
        for k in range(3):
            term = weights[k] * (value[k] * value[k] + value[k + 3] * value[k + 3])
            total = term if total is None else total + term
        return total

    halves = (slice(0, R), slice(R, T))
    sums = []
    for i in range(4):
        ipart[i] = amplitudes(i)
        for half in range(2):
            n = 2 * i + half
            copy = remote(ipart.at[i, :, halves[half]], ione.at[n], isend.at[n], isem.at[n], {"kern": pair[half]})
            copy.start()
            sums.append(copy)
    shares = []
    for i in range(4):
        for half in range(2):
            n = 2 * i + half
            sums[n].wait_recv()
            imid[n] = ipart[i, :, halves[half]] + ione[n]
            copy = remote(imid.at[n], itwo.at[n], asend.at[n], asem.at[n], {"kern": pair[1 - half]})
            copy.start()
            shares.append(copy)

    loads[5].wait()
    for i in range(4):
        at = rows_of(i)
        for half in range(2):
            shares[2 * i + half].wait_recv()
        intensity = jnp.concatenate([imid[2 * i] + itwo[2 * i], imid[2 * i + 1] + itwo[2 * i + 1]], axis=1) * (1.0 / 12.0)
        x = 1.0 / (1.0 + jnp.exp(-8.0 * (intensity - 0.25)))
        resv[at, :] = x
        factor = 2.0 * (x - targ[at, :].astype(F32)) * 8.0 * x * (1.0 - x)
        both = [split(factor * (weights[a % 3] * (2.0 / 12.0)) * amp[a, at, :]) for a in range(PARTS)]
        h_ = jnp.concatenate([x[0] for x in both], axis=0)
        l_ = jnp.concatenate([x[1] for x in both], axis=0)
        for b in range(2):
            cut = slice(b * T, b * T + T)
            u, v = split(dot3(h_, l_, rh[:T, cut], rl[:T, cut]).reshape(PARTS, Q, T))
            ph[:, at, cut] = u
            pw[:, at, cut] = v
    store = pltpu.make_async_copy(resv, resist, lsem.at[7])
    store.start()

    firsts = []
    for b in range(2):
        at = slice(b * T, b * T + T)
        acc[...] = jnp.zeros_like(acc)

        def gather(a, carry, at=at, b=b):
            value = dot3(th[:, :T], tl[:, :T], ph[a, :, at], pw[a, :, at])
            for f in range(2):
                p = to_complex(value[f * T:f * T + T])
                fr = slice(f * R, f * R + R)
                h = [hs[a, n, fr, b * R:b * R + R] for n in range(4)]
                for n in (0, 2):
                    acc[n, fr, :] += p[n] * h[n] - p[n + 1] * h[n + 1]
                    acc[n + 1, fr, :] += p[n] * h[n + 1] + p[n + 1] * h[n]
            return carry

        loop(0, PARTS, gather, 0)
        for f in range(2):
            fr = slice(f * R, f * R + R)
            for n, x in enumerate(from_complex(*[acc[i, fr, :] for i in range(4)])):
                h_, l_ = split(x)
                to = (slice(f * T + (n // 2) * R, f * T + (n // 2) * R + R),
                      slice(b * T + (n % 2) * R, b * T + (n % 2) * R + R))
                xh[to[0], to[1]] = h_
                xl[to[0], to[1]] = l_
        value = dot3(rh[...], rl[...], xh[:, at], xl[:, at])
        for q in range(4):
            for far in range(2):
                m = (q + 6) % 8 if far == 0 else q + 2
                tsend[b, q, far] = value[m * Q:m * Q + Q]
        for half in range(2):
            to = pair[half]
            for slot, owner in enumerate((to, partner(1 - half, to))):
                n = (b * 2 + half) * 2 + slot
                copy = remote(tsend.at[b, owner, :, :, half * R:half * R + R], tone.at[n],
                              tss.at[n], trs.at[n], {"kern": to})
                copy.start()
                firsts.append(copy)

    seconds = []
    for b in range(2):
        for half in range(2):
            n = b * 2 + half
            firsts[2 * n].wait_recv()
            firsts[2 * n + 1].wait_recv()
            to = pair[1 - half]
            tmid[n] = tsend[b, to, :, :, half * R:half * R + R] + tone[2 * n + 1]
            copy = remote(tmid.at[n], ttwo.at[n], uss.at[n], urs.at[n], {"kern": to})
            copy.start()
            seconds.append(copy)

    for b in range(2):
        for half in range(2):
            n = b * 2 + half
            seconds[n].wait_recv()
            part = tsend[b, j, :, :, half * R:half * R + R] + tone[2 * n] + ttwo[n]
            gw[:, b * T + half * R:b * T + half * R + R] = part.reshape(2 * Q, R)
    g_h, g_l = split(gw[...])
    gw[...] = dot3(g_h, g_l, th[...], tl[...])
    far_rows, near_rows = slice(0, Q), slice(Q, 2 * Q)
    west, east = exists(0, -1), exists(0, 1)
    ends = [
        (gives, takes, gw.at[far_rows, mid], ecen, device(step, 0)),
        (jnp.logical_and(gives, west), jnp.logical_and(takes, east), gw.at[far_rows, low], eside.at[0], device(step, -1)),
        (jnp.logical_and(gives, east), jnp.logical_and(takes, west), gw.at[far_rows, high], eside.at[1], device(step, 1)),
        (west, east, gw.at[near_rows, low], eside.at[2], device(0, -1)),
        (east, west, gw.at[near_rows, high], eside.at[3], device(0, 1)),
    ]
    hops = [remote(src, dst, ess.at[n], ers.at[n], to) for n, (_, _, src, dst, to) in enumerate(ends)]
    for n in range(5):
        pl.when(ends[n][0])(hops[n].start)
    lane = lax.broadcasted_iota(jnp.int32, (1, T), 1) // 64
    pixels = jnp.zeros((1, T), F32)
    for k in range(4):
        pixels = jnp.where(lane == k, active[j, k].astype(F32), pixels)
    pixels = pixels * SCALE
    for n in range(5):
        pl.when(ends[n][1])(hops[n].wait_recv)
    own_part = gw[near_rows, mid] + ecen[...]
    outv[:, :R] = (own_part[:, :R] + eside[1] + eside[3]) * pixels[:, :R]
    outv[:, R:] = (own_part[:, R:] + eside[0] + eside[2]) * pixels[:, R:]

    final = pltpu.make_async_copy(outv, gradient, lsem.at[0])
    final.start()

    for n in range(8):
        pl.when(exists(*pieces[n][:2]))(copies[n].wait_send)
    for n in range(2):
        for d in range(3):
            pl.when(exists(-pieces[n][0], 0))(passes[d][n].wait_send)
    for copy in sums + shares + firsts + seconds:
        copy.wait_send()
    for n in range(5):
        pl.when(ends[n][0])(hops[n].wait_send)
    store.wait()
    final.wait()


def local(photomask, target_bits, active_blocks, kernel_taps, kernel_weights):
    hbm = pl.BlockSpec(memory_space=pl.ANY)
    smem = pl.BlockSpec(memory_space=pltpu.SMEM)
    vmem = pltpu.VMEM
    dma = pltpu.SemaphoreType.DMA
    scratch = [
        vmem((W, W), F32),
        vmem((2, 3, 2 * R + 1, 2 * R + 1), F32),
        vmem((W, W), BF), vmem((W, W), BF), vmem((W, W), BF), vmem((W, W), BF),
        vmem((T, T), jnp.int32),
        vmem((8, T), F32),
        vmem((8, W), F32),
        vmem((W, W), BF), vmem((W, W), BF),
        vmem((W, W), F32),
        vmem((PARTS, 4, T, T), F32),
        vmem((4, T, T), F32),
        vmem((PARTS, T, W), BF), vmem((PARTS, T, W), BF),
        vmem((PARTS, T, T), F32),
        vmem((PARTS, T, W), BF), vmem((PARTS, T, W), BF),
        vmem((4, Q, T), F32), vmem((8, Q, R), F32), vmem((8, Q, R), F32), vmem((8, Q, R), F32),
        vmem((T, T), F32),
        vmem((4, T, R), F32),
        vmem((2, 4, 2, Q, T), F32),
        vmem((8, 2, Q, R), F32), vmem((4, 2, Q, R), F32), vmem((4, 2, Q, R), F32),
        vmem((2 * Q, W), F32),
        vmem((Q, T), F32), vmem((4, Q, R), F32),
        vmem((Q, T), F32),
        dma((14,)), dma((8,)), dma((8,)),
        dma((6,)), dma((6,)),
        dma((8,)), dma((8,)), dma((8,)), dma((8,)),
        dma((8,)), dma((8,)), dma((4,)), dma((4,)),
        dma((5,)), dma((5,)),
    ]
    outs = (jax.ShapeDtypeStruct((Q, T), F32), jax.ShapeDtypeStruct((T, T), F32))
    gradient, resist = pl.pallas_call(
        kernel,
        out_shape=outs,
        in_specs=[hbm, hbm, smem, hbm, smem, hbm, hbm, hbm, hbm],
        out_specs=(hbm, hbm),
        scratch_shapes=scratch,
        compiler_params=pltpu.CompilerParams(
            collective_id=0, has_side_effects=True, vmem_limit_bytes=56 * 1024 * 1024),
        name="socs",
    )(photomask, target_bits, active_blocks, kernel_taps.transpose(1, 2, 0, 3), kernel_weights,
      *[jnp.asarray(t) for t in tables()])
    return pl.pallas_call(hand_over, out_shape=outs, name="hand_over")(gradient, resist)


def solution(mesh):
    in_specs = (
        P("row", "col"),
        P("row", "col"),
        P("row", "col"),
        P(None, "kern", None, None),
        P("kern"),
    )
    out_specs = (P(("row", "kern"), "col"), P("row", "col"))
    return jax.shard_map(local, mesh=mesh, in_specs=in_specs, out_specs=out_specs, check_vma=False)
```

```python
import functools

import jax
import jax.numpy as jnp
import numpy as np
from jax import lax
from jax.experimental import pallas as pl
from jax.experimental.pallas import tpu as pltpu
from jax.sharding import PartitionSpec as P

MESH = pl.DeviceIdType.MESH
T = 256
W = 512
R = 128
PARTS = 6
Q = 64
SCALE = 2.0 ** -17
F32 = jnp.float32
BF = jnp.bfloat16


def tables():
    sample = np.arange(W)[:, None]
    freq = np.arange(T)[None, :]
    angle = np.pi / W * (sample * (2 * freq + 1) % (2 * W))
    cos, sin = np.cos(angle), np.sin(angle)
    full = np.concatenate([cos[:, :R], sin[:, :R], cos[:, R:], sin[:, R:]], axis=1)
    full[np.abs(full) < 1e-12] = 0.0
    high = full.astype(BF)
    low = (full - high.astype(np.float64)).astype(BF)
    return high, low, np.ascontiguousarray(high.T), np.ascontiguousarray(low.T)


def split(value):
    high = value.astype(BF)
    return high, (value - high.astype(F32)).astype(BF)


def dot(a, b):
    return jnp.dot(a, b, preferred_element_type=F32)


def dot3(ah, al, bh, bl):
    return dot(ah, bh) + dot(al, bh) + dot(ah, bl)


def to_complex(block):
    cc, cs = block[:R, :R], block[:R, R:]
    sc, ss = block[R:, :R], block[R:, R:]
    return cc - ss, -(cs + sc), cc + ss, cs - sc


def from_complex(pr, pi, mr, mi):
    return pr + mr, mi - pi, -(pi + mi), mr - pr


def loop(lo, hi, fn, init):
    for i in range(lo, hi):
        fn(i, init)


def spectrum_block(quads):
    rows = []
    for cc, cs, sc, ss in quads:
        rows += [jnp.concatenate([cc, cs], axis=1), jnp.concatenate([sc, ss], axis=1)]
    return split(jnp.concatenate(rows, axis=0))


def kernel(
    mask, target, active, taps, weights, rh_in, rl_in, th_in, tl_in,
    gradient, resist,
    win, tapv, rh, rl, th, tl, targ, taph, rhat, xh, xl, mpart, hs, ms, vh, vl, amp, ph, pw,
    ipart, ione, imid, itwo, acc, tsend, tone, tmid, ttwo, gw, ecen, eside,
    lsem, msend, mrecv, psend, precv, isend, isem, asend, asem, tss, trs, uss, urs, ess, ers,
):
    r, c, j = lax.axis_index("row"), lax.axis_index("col"), lax.axis_index("kern")
    rows, cols = lax.axis_size("row"), lax.axis_size("col")
    def exists(dr, dc):
        ok = None
        for at, d, n in ((r, dr, rows), (c, dc, cols)):
            if d:
                one = at > 0 if d < 0 else at < n - 1
                ok = one if ok is None else jnp.logical_and(ok, one)
        return ok

    def device(dr, dc):
        return {"row": r + dr, "col": c + dc}

    around = [(dr, dc) for dr in (-1, 0, 1) for dc in (-1, 0, 1) if dr or dc]
    down = j < 2
    step = jnp.where(down, 1, -1)
    gives = jnp.logical_or(jnp.logical_and(down, r < rows - 1), jnp.logical_and(jnp.logical_not(down), r > 0))
    takes = jnp.logical_or(jnp.logical_and(down, r > 0), jnp.logical_and(jnp.logical_not(down), r < rows - 1))
    peer = [lax.rem(j + d, 4) for d in range(4)]

    ecen[...] = jnp.zeros_like(ecen)
    eside[...] = jnp.zeros_like(eside)
    barrier = pltpu.get_barrier_semaphore()
    count = 3
    for dr, dc in around:
        ok = exists(dr, dc)
        count = count + ok.astype(jnp.int32)

        @pl.when(ok)
        def _(dr=dr, dc=dc):
            pl.semaphore_signal(barrier, inc=1, device_id=device(dr, dc), device_id_type=MESH)
    for d in range(1, 4):
        pl.semaphore_signal(barrier, inc=1, device_id={"kern": peer[d]}, device_id_type=MESH)
    loads = [
        pltpu.make_async_copy(mask, win.at[R:R + T, R:R + T], lsem.at[0]),
        pltpu.make_async_copy(rh_in, rh, lsem.at[1]),
        pltpu.make_async_copy(rl_in, rl, lsem.at[2]),
        pltpu.make_async_copy(th_in, th, lsem.at[3]),
        pltpu.make_async_copy(tl_in, tl, lsem.at[4]),
        pltpu.make_async_copy(target, targ, lsem.at[5]),
    ]
    loads += [
        pltpu.make_async_copy(taps.at[a % 3, :, a // 3, :], tapv.at[a // 3, a % 3], lsem.at[8 + a])
        for a in range(PARTS)
    ]
    for load in loads:
        load.start()

    @pl.when(r == 0)
    def _():
        win[:R, :] = jnp.zeros((R, W), F32)

    @pl.when(r == rows - 1)
    def _():
        win[R + T:, :] = jnp.zeros((R, W), F32)

    @pl.when(c == 0)
    def _():
        win[:, :R] = jnp.zeros((W, R), F32)

    @pl.when(c == cols - 1)
    def _():
        win[:, R + T:] = jnp.zeros((W, R), F32)

    pl.semaphore_wait(barrier, count)

    def remote(src, dst, s, d, to):
        return pltpu.make_async_remote_copy(
            src_ref=src, dst_ref=dst, send_sem=s, recv_sem=d, device_id=to, device_id_type=MESH)

    low, mid, high = slice(0, R), slice(R, R + T), slice(R + T, W)
    part_rows = R // 4

    def quarter(start, q):
        return pl.ds(pl.multiple_of(start + q * part_rows, part_rows), part_rows)

    pieces = [
        (-1, 0, mask.at[quarter(0, j), :], win.at[quarter(R + T, j), mid]),
        (1, 0, mask.at[quarter(R, j), :], win.at[quarter(0, j), mid]),
        (0, -1, mask.at[:, 0:R], win.at[mid, high]),
        (0, 1, mask.at[:, R:T], win.at[mid, low]),
        (-1, -1, mask.at[0:R, 0:R], win.at[high, high]),
        (-1, 1, mask.at[0:R, R:T], win.at[high, low]),
        (1, -1, mask.at[R:T, 0:R], win.at[low, high]),
        (1, 1, mask.at[R:T, R:T], win.at[low, low]),
    ]
    copies = [remote(src, dst, msend.at[n], mrecv.at[n], device(dr, dc))
              for n, (dr, dc, src, dst) in enumerate(pieces)]
    for n in range(8):
        pl.when(exists(*pieces[n][:2]))(copies[n].start)

    def arrived(n):
        pl.when(exists(-pieces[n][0], -pieces[n][1]))(copies[n].wait_recv)

    def passed(d):
        return [
            remote(win.at[quarter(start, j), mid], win.at[quarter(start, j), mid],
                   psend.at[2 * d - 2 + n], precv.at[2 * d - 2 + n], {"kern": peer[d]})
            for n, start in enumerate((R + T, 0))
        ]

    passes = [passed(d) for d in range(1, 4)]

    for load in loads[1:5] + loads[6:]:
        load.wait()
    sign_row = (1 - 2 * (lax.broadcasted_iota(jnp.int32, (1, R), 1) & 1)).astype(F32)
    sign_col = (1 - 2 * (lax.broadcasted_iota(jnp.int32, (R, 1), 0) & 1)).astype(F32)
    taph[...] = jnp.zeros_like(taph)
    for a in range(PARTS):
        taph[a:a + 1, :] = tapv[a // 3, a % 3, T:T + 1, 0:T]
    edge_h, edge_l = split(taph[...])
    rhat[...] = dot3(edge_h, edge_l, rh[:T, :], rl[:T, :])
    for a in range(PARTS):
        corner = tapv[a // 3, a % 3, T:T + 1, T:T + 1]
        for b in range(2):
            at = slice(b * T + R, b * T + T)
            rhat[a:a + 1, at] = rhat[a:a + 1, at] + corner * sign_row

    def tap_spectrum(a, carry):
        part, k = a // 3, a % 3
        low_h, low_l = split(tapv[part, k, 0:T, 0:T])
        column = tapv[part, k, 0:T, T:T + 1]
        for b in range(2):
            at = slice(b * T, b * T + T)
            value = dot3(low_h, low_l, rh[:T, at], rl[:T, at])
            value = jnp.concatenate([value[:, :R], value[:, R:] + column * sign_row], axis=1)
            vh_, vl_ = split(value)
            xh[:T, at] = vh_
            xl[:T, at] = vl_
        for b in range(2):
            at = slice(b * T, b * T + T)
            value = dot3(th[:, :T], tl[:, :T], xh[:T, at], xl[:T, at])
            edge = sign_col * rhat[a:a + 1, at]
            for f in range(2):
                block = value[f * T:f * T + T]
                block = jnp.concatenate([block[:R], block[R:] + edge], axis=0)
                for n, x in enumerate(to_complex(block)):
                    hs[a, n, f * R:f * R + R, b * R:b * R + R] = x
        return carry

    loop(0, 4, tap_spectrum, 0)

    for n in range(2):
        arrived(n)
        for d in range(3):
            pl.when(exists(-pieces[n][0], 0))(passes[d][n].start)

    loop(4, PARTS, tap_spectrum, 0)

    loads[0].wait()
    for n in (2, 3):
        arrived(n)

    def mask_columns(values):
        h_, l_ = split(values)
        return [split(dot3(h_, l_, rh[:, b * T:b * T + T], rl[:, b * T:b * T + T])) for b in range(2)]

    for b, (h_, l_) in enumerate(mask_columns(win[mid, :])):
        mpart[:, b * T:b * T + T] = dot3(th[:, mid], tl[:, mid], h_, l_)

    for n in range(4, 8):
        arrived(n)
    for d in range(1, 4):
        q = lax.rem(j + 4 - d, 4)
        for n, start in enumerate((R + T, 0)):
            at = win.at[quarter(start, q), mid]
            came = remote(at, at, psend.at[2 * d - 2 + n], precv.at[2 * d - 2 + n], {"kern": peer[d]})
            pl.when(exists(-pieces[n][0], 0))(came.wait_recv)

    outer = [jnp.concatenate([t[:, low], t[:, high]], axis=1) for t in (th, tl)]
    for b, (h_, l_) in enumerate(mask_columns(jnp.concatenate([win[low, :], win[high, :]], axis=0))):
        value = mpart[:, b * T:b * T + T] + dot3(*outer, h_, l_)
        for f in range(2):
            for n, x in enumerate(to_complex(value[f * T:f * T + T])):
                ms[n, f * R:f * R + R, b * R:b * R + R] = x

    def inverse_rows(a, carry):
        for b in range(2):
            quads = []
            for f in range(2):
                at = (slice(f * R, f * R + R), slice(b * R, b * R + R))
                m = [ms[n, at[0], at[1]] for n in range(4)]
                h = [hs[a, n, at[0], at[1]] for n in range(4)]
                y = []
                for n in (0, 2):
                    y.append(m[n] * h[n] + m[n + 1] * h[n + 1])
                    y.append(m[n + 1] * h[n] - m[n] * h[n + 1])
                quads.append(from_complex(*y))
            at = slice(b * T, b * T + T)
            h_, l_ = split(dot3(rh[:T, :], rl[:T, :], *spectrum_block(quads)))
            vh[a, :, at] = h_
            vl[a, :, at] = l_
        return carry

    loop(0, PARTS, inverse_rows, 0)

    def partner(kind, at):
        return at + 1 - 2 * lax.rem(at, 2) if kind == 0 else 3 - at

    pair = (partner(0, j), partner(1, j))
    def rows_of(i):
        return slice(i * Q, i * Q + Q)

    def amplitudes(i):
        at = rows_of(i)
        value = dot3(vh[:, at, :].reshape(PARTS * Q, W), vl[:, at, :].reshape(PARTS * Q, W),
                     th[:, :T], tl[:, :T]).reshape(PARTS, Q, T) * SCALE
        amp[:, at, :] = value
        total = None
        for k in range(3):
            term = weights[k] * (value[k] * value[k] + value[k + 3] * value[k + 3])
            total = term if total is None else total + term
        return total

    halves = (slice(0, R), slice(R, T))
    sums = []
    for i in range(4):
        ipart[i] = amplitudes(i)
        for half in range(2):
            n = 2 * i + half
            copy = remote(ipart.at[i, :, halves[half]], ione.at[n], isend.at[n], isem.at[n], {"kern": pair[half]})
            copy.start()
            sums.append(copy)
    shares = []
    for i in range(4):
        for half in range(2):
            n = 2 * i + half
            sums[n].wait_recv()
            imid[n] = ipart[i, :, halves[half]] + ione[n]
            copy = remote(imid.at[n], itwo.at[n], asend.at[n], asem.at[n], {"kern": pair[1 - half]})
            copy.start()
            shares.append(copy)

    loads[5].wait()
    for i in range(4):
        at = rows_of(i)
        for half in range(2):
            shares[2 * i + half].wait_recv()
        intensity = jnp.concatenate([imid[2 * i] + itwo[2 * i], imid[2 * i + 1] + itwo[2 * i + 1]], axis=1) * (1.0 / 12.0)
        x = 1.0 / (1.0 + jnp.exp(-8.0 * (intensity - 0.25)))
        resist[at, :] = x
        factor = 2.0 * (x - targ[at, :].astype(F32)) * 8.0 * x * (1.0 - x)
        both = [split(factor * (weights[a % 3] * (2.0 / 12.0)) * amp[a, at, :]) for a in range(PARTS)]
        h_ = jnp.concatenate([x[0] for x in both], axis=0)
        l_ = jnp.concatenate([x[1] for x in both], axis=0)
        for b in range(2):
            cut = slice(b * T, b * T + T)
            u, v = split(dot3(h_, l_, rh[:T, cut], rl[:T, cut]).reshape(PARTS, Q, T))
            ph[:, at, cut] = u
            pw[:, at, cut] = v

    firsts = []
    for b in range(2):
        at = slice(b * T, b * T + T)
        acc[...] = jnp.zeros_like(acc)

        def gather(a, carry, at=at, b=b):
            value = dot3(th[:, :T], tl[:, :T], ph[a, :, at], pw[a, :, at])
            for f in range(2):
                p = to_complex(value[f * T:f * T + T])
                fr = slice(f * R, f * R + R)
                h = [hs[a, n, fr, b * R:b * R + R] for n in range(4)]
                for n in (0, 2):
                    acc[n, fr, :] += p[n] * h[n] - p[n + 1] * h[n + 1]
                    acc[n + 1, fr, :] += p[n] * h[n + 1] + p[n + 1] * h[n]
            return carry

        loop(0, PARTS, gather, 0)
        quads = [from_complex(*[acc[i, f * R:f * R + R, :] for i in range(4)]) for f in range(2)]
        value = dot3(rh[...], rl[...], *spectrum_block(quads))
        for q in range(4):
            for far in range(2):
                m = (q + 6) % 8 if far == 0 else q + 2
                tsend[b, q, far] = value[m * Q:m * Q + Q]
        for half in range(2):
            to = pair[half]
            for slot, owner in enumerate((to, partner(1 - half, to))):
                n = (b * 2 + half) * 2 + slot
                copy = remote(tsend.at[b, owner, :, :, half * R:half * R + R], tone.at[n],
                              tss.at[n], trs.at[n], {"kern": to})
                copy.start()
                firsts.append(copy)

    seconds = []
    for b in range(2):
        for half in range(2):
            n = b * 2 + half
            firsts[2 * n].wait_recv()
            firsts[2 * n + 1].wait_recv()
            to = pair[1 - half]
            tmid[n] = tsend[b, to, :, :, half * R:half * R + R] + tone[2 * n + 1]
            copy = remote(tmid.at[n], ttwo.at[n], uss.at[n], urs.at[n], {"kern": to})
            copy.start()
            seconds.append(copy)

    for b in range(2):
        for half in range(2):
            n = b * 2 + half
            seconds[n].wait_recv()
            part = tsend[b, j, :, :, half * R:half * R + R] + tone[2 * n] + ttwo[n]
            gw[:, b * T + half * R:b * T + half * R + R] = part.reshape(2 * Q, R)
    g_h, g_l = split(gw[...])
    gw[...] = dot3(g_h, g_l, th[...], tl[...])
    far_rows, near_rows = slice(0, Q), slice(Q, 2 * Q)
    west, east = exists(0, -1), exists(0, 1)
    ends = [
        (gives, takes, gw.at[far_rows, mid], ecen, device(step, 0)),
        (jnp.logical_and(gives, west), jnp.logical_and(takes, east), gw.at[far_rows, low], eside.at[0], device(step, -1)),
        (jnp.logical_and(gives, east), jnp.logical_and(takes, west), gw.at[far_rows, high], eside.at[1], device(step, 1)),
        (west, east, gw.at[near_rows, low], eside.at[2], device(0, -1)),
        (east, west, gw.at[near_rows, high], eside.at[3], device(0, 1)),
    ]
    hops = [remote(src, dst, ess.at[n], ers.at[n], to) for n, (_, _, src, dst, to) in enumerate(ends)]
    for n in range(5):
        pl.when(ends[n][0])(hops[n].start)
    lane = lax.broadcasted_iota(jnp.int32, (1, T), 1) // 64
    pixels = jnp.zeros((1, T), F32)
    for k in range(4):
        pixels = jnp.where(lane == k, active[j, k].astype(F32), pixels)
    pixels = pixels * SCALE
    for n in range(5):
        pl.when(ends[n][1])(hops[n].wait_recv)
    own_part = gw[near_rows, mid] + ecen[...]
    gradient[:, :R] = (own_part[:, :R] + eside[1] + eside[3]) * pixels[:, :R]
    gradient[:, R:] = (own_part[:, R:] + eside[0] + eside[2]) * pixels[:, R:]


    for n in range(8):
        pl.when(exists(*pieces[n][:2]))(copies[n].wait_send)
    for n in range(2):
        for d in range(3):
            pl.when(exists(-pieces[n][0], 0))(passes[d][n].wait_send)
    for copy in sums + shares + firsts + seconds:
        copy.wait_send()
    for n in range(5):
        pl.when(ends[n][0])(hops[n].wait_send)


def local(photomask, target_bits, active_blocks, kernel_taps, kernel_weights):
    hbm = pl.BlockSpec(memory_space=pl.ANY)
    smem = pl.BlockSpec(memory_space=pltpu.SMEM)
    vmem = pltpu.VMEM
    dma = pltpu.SemaphoreType.DMA
    scratch = [
        vmem((W, W), F32),
        vmem((2, 3, 2 * R + 1, 2 * R + 1), F32),
        vmem((W, W), BF), vmem((W, W), BF), vmem((W, W), BF), vmem((W, W), BF),
        vmem((T, T), jnp.int32),
        vmem((8, T), F32),
        vmem((8, W), F32),
        vmem((W, W), BF), vmem((W, W), BF),
        vmem((W, W), F32),
        vmem((PARTS, 4, T, T), F32),
        vmem((4, T, T), F32),
        vmem((PARTS, T, W), BF), vmem((PARTS, T, W), BF),
        vmem((PARTS, T, T), F32),
        vmem((PARTS, T, W), BF), vmem((PARTS, T, W), BF),
        vmem((4, Q, T), F32), vmem((8, Q, R), F32), vmem((8, Q, R), F32), vmem((8, Q, R), F32),
        vmem((4, T, R), F32),
        vmem((2, 4, 2, Q, T), F32),
        vmem((8, 2, Q, R), F32), vmem((4, 2, Q, R), F32), vmem((4, 2, Q, R), F32),
        vmem((2 * Q, W), F32),
        vmem((Q, T), F32), vmem((4, Q, R), F32),
        dma((14,)), dma((8,)), dma((8,)),
        dma((6,)), dma((6,)),
        dma((8,)), dma((8,)), dma((8,)), dma((8,)),
        dma((8,)), dma((8,)), dma((4,)), dma((4,)),
        dma((5,)), dma((5,)),
    ]
    return pl.pallas_call(
        kernel,
        out_shape=(vmem((Q, T), F32), vmem((T, T), F32)),
        in_specs=[hbm, hbm, smem, hbm, smem, hbm, hbm, hbm, hbm],
        out_specs=(pl.BlockSpec(memory_space=vmem), pl.BlockSpec(memory_space=vmem)),
        scratch_shapes=scratch,
        compiler_params=pltpu.CompilerParams(
            collective_id=0, has_side_effects=True, vmem_limit_bytes=56 * 1024 * 1024),
        name="socs",
    )(photomask, target_bits, active_blocks, kernel_taps.transpose(1, 2, 0, 3), kernel_weights,
      *[jnp.asarray(t) for t in tables()])


def solution(mesh):
    in_specs = (
        P("row", "col"),
        P("row", "col"),
        P("row", "col"),
        P(None, "kern", None, None),
        P("kern"),
    )
    out_specs = (P(("row", "kern"), "col"), P("row", "col"))
    return jax.shard_map(local, mesh=mesh, in_specs=in_specs, out_specs=out_specs, check_vma=False)
```

```python
import functools

import jax
import jax.numpy as jnp
import numpy as np
from jax import lax
from jax.experimental import pallas as pl
from jax.experimental.pallas import tpu as pltpu
from jax.sharding import PartitionSpec as P

MESH = pl.DeviceIdType.MESH
T = 256
W = 512
R = 128
PARTS = 6
Q = 64
SCALE = 2.0 ** -17
F32 = jnp.float32
BF = jnp.bfloat16


def tables():
    sample = np.arange(W)[:, None]
    freq = np.arange(T)[None, :]
    angle = np.pi / W * (sample * (2 * freq + 1) % (2 * W))
    cos, sin = np.cos(angle), np.sin(angle)
    full = np.concatenate([cos[:, :R], sin[:, :R], cos[:, R:], sin[:, R:]], axis=1)
    full[np.abs(full) < 1e-12] = 0.0
    high = full.astype(BF)
    low = (full - high.astype(np.float64)).astype(BF)
    return high, low, np.ascontiguousarray(high.T), np.ascontiguousarray(low.T)


def split(value):
    high = value.astype(BF)
    return high, (value - high.astype(F32)).astype(BF)


def dot(a, b):
    return jnp.dot(a, b, preferred_element_type=F32)


def dot3(ah, al, bh, bl):
    return dot(ah, bh) + dot(al, bh) + dot(ah, bl)


def to_complex(block):
    cc, cs = block[:R, :R], block[:R, R:]
    sc, ss = block[R:, :R], block[R:, R:]
    return cc - ss, -(cs + sc), cc + ss, cs - sc


def from_complex(pr, pi, mr, mi):
    return pr + mr, mi - pi, -(pi + mi), mr - pr


def loop(lo, hi, fn, init):
    for i in range(lo, hi):
        fn(i, init)


def spectrum_block(quads):
    rows = []
    for cc, cs, sc, ss in quads:
        rows += [jnp.concatenate([cc, cs], axis=1), jnp.concatenate([sc, ss], axis=1)]
    return split(jnp.concatenate(rows, axis=0))


def kernel(
    mask, target, active, taps, weights, rh_in, rl_in, th_in, tl_in,
    gradient, resist,
    win, tapv, rh, rl, th, tl, targ, taph, rhat, xh, xl, mpart, hs, ms, vh, vl, amp, ph, pw,
    ipart, ione, imid, itwo, acc, tsend, tone, tmid, ttwo, gw, ecen, eside,
    lsem, msend, mrecv, psend, precv, isend, isem, asend, asem, tss, trs, uss, urs, ess, ers,
):
    r, c, j = lax.axis_index("row"), lax.axis_index("col"), lax.axis_index("kern")
    rows, cols = lax.axis_size("row"), lax.axis_size("col")
    def exists(dr, dc):
        ok = None
        for at, d, n in ((r, dr, rows), (c, dc, cols)):
            if d:
                one = at > 0 if d < 0 else at < n - 1
                ok = one if ok is None else jnp.logical_and(ok, one)
        return ok

    def device(dr, dc):
        return {"row": r + dr, "col": c + dc}

    around = [(dr, dc) for dr in (-1, 0, 1) for dc in (-1, 0, 1) if dr or dc]
    down = j < 2
    step = jnp.where(down, 1, -1)
    gives = jnp.logical_or(jnp.logical_and(down, r < rows - 1), jnp.logical_and(jnp.logical_not(down), r > 0))
    takes = jnp.logical_or(jnp.logical_and(down, r > 0), jnp.logical_and(jnp.logical_not(down), r < rows - 1))
    peer = [lax.rem(j + d, 4) for d in range(4)]

    ecen[...] = jnp.zeros_like(ecen)
    eside[...] = jnp.zeros_like(eside)
    barrier = pltpu.get_barrier_semaphore()
    count = 3
    for dr, dc in around:
        ok = exists(dr, dc)
        count = count + ok.astype(jnp.int32)

        @pl.when(ok)
        def _(dr=dr, dc=dc):
            pl.semaphore_signal(barrier, inc=1, device_id=device(dr, dc), device_id_type=MESH)
    for d in range(1, 4):
        pl.semaphore_signal(barrier, inc=1, device_id={"kern": peer[d]}, device_id_type=MESH)
    loads = [
        pltpu.make_async_copy(mask, win.at[R:R + T, R:R + T], lsem.at[0]),
        pltpu.make_async_copy(rh_in, rh, lsem.at[1]),
        pltpu.make_async_copy(rl_in, rl, lsem.at[2]),
        pltpu.make_async_copy(th_in, th, lsem.at[3]),
        pltpu.make_async_copy(tl_in, tl, lsem.at[4]),
        pltpu.make_async_copy(target, targ, lsem.at[5]),
    ]
    loads += [
        pltpu.make_async_copy(taps.at[a % 3, :, a // 3, :], tapv.at[a // 3, a % 3], lsem.at[8 + a])
        for a in range(PARTS)
    ]
    for load in loads:
        load.start()

    @pl.when(r == 0)
    def _():
        win[:R, :] = jnp.zeros((R, W), F32)

    @pl.when(r == rows - 1)
    def _():
        win[R + T:, :] = jnp.zeros((R, W), F32)

    @pl.when(c == 0)
    def _():
        win[:, :R] = jnp.zeros((W, R), F32)

    @pl.when(c == cols - 1)
    def _():
        win[:, R + T:] = jnp.zeros((W, R), F32)

    pl.semaphore_wait(barrier, count)

    def remote(src, dst, s, d, to):
        return pltpu.make_async_remote_copy(
            src_ref=src, dst_ref=dst, send_sem=s, recv_sem=d, device_id=to, device_id_type=MESH)

    low, mid, high = slice(0, R), slice(R, R + T), slice(R + T, W)
    part_rows = R // 4

    def quarter(start, q):
        return pl.ds(pl.multiple_of(start + q * part_rows, part_rows), part_rows)

    pieces = [
        (-1, 0, mask.at[quarter(0, j), :], win.at[quarter(R + T, j), mid]),
        (1, 0, mask.at[quarter(R, j), :], win.at[quarter(0, j), mid]),
        (0, -1, mask.at[:, 0:R], win.at[mid, high]),
        (0, 1, mask.at[:, R:T], win.at[mid, low]),
        (-1, -1, mask.at[0:R, 0:R], win.at[high, high]),
        (-1, 1, mask.at[0:R, R:T], win.at[high, low]),
        (1, -1, mask.at[R:T, 0:R], win.at[low, high]),
        (1, 1, mask.at[R:T, R:T], win.at[low, low]),
    ]
    copies = [remote(src, dst, msend.at[n], mrecv.at[n], device(dr, dc))
              for n, (dr, dc, src, dst) in enumerate(pieces)]
    for n in range(8):
        pl.when(exists(*pieces[n][:2]))(copies[n].start)

    def arrived(n):
        pl.when(exists(-pieces[n][0], -pieces[n][1]))(copies[n].wait_recv)

    def passed(d):
        return [
            remote(win.at[quarter(start, j), mid], win.at[quarter(start, j), mid],
                   psend.at[2 * d - 2 + n], precv.at[2 * d - 2 + n], {"kern": peer[d]})
            for n, start in enumerate((R + T, 0))
        ]

    passes = [passed(d) for d in range(1, 4)]

    for load in loads[1:5] + loads[6:]:
        load.wait()
    sign_row = (1 - 2 * (lax.broadcasted_iota(jnp.int32, (1, R), 1) & 1)).astype(F32)
    sign_col = (1 - 2 * (lax.broadcasted_iota(jnp.int32, (R, 1), 0) & 1)).astype(F32)
    taph[...] = jnp.zeros_like(taph)
    for a in range(PARTS):
        taph[a:a + 1, :] = tapv[a // 3, a % 3, T:T + 1, 0:T]
    edge_h, edge_l = split(taph[...])
    rhat[...] = dot3(edge_h, edge_l, rh[:T, :], rl[:T, :])
    for a in range(PARTS):
        corner = tapv[a // 3, a % 3, T:T + 1, T:T + 1]
        for b in range(2):
            at = slice(b * T + R, b * T + T)
            rhat[a:a + 1, at] = rhat[a:a + 1, at] + corner * sign_row

    def tap_spectrum(a, carry):
        part, k = a // 3, a % 3
        low_h, low_l = split(tapv[part, k, 0:T, 0:T])
        column = tapv[part, k, 0:T, T:T + 1]
        for b in range(2):
            at = slice(b * T, b * T + T)
            value = dot3(low_h, low_l, rh[:T, at], rl[:T, at])
            value = jnp.concatenate([value[:, :R], value[:, R:] + column * sign_row], axis=1)
            vh_, vl_ = split(value)
            xh[:T, at] = vh_
            xl[:T, at] = vl_
        for b in range(2):
            at = slice(b * T, b * T + T)
            value = dot3(th[:, :T], tl[:, :T], xh[:T, at], xl[:T, at])
            edge = sign_col * rhat[a:a + 1, at]
            for f in range(2):
                block = value[f * T:f * T + T]
                block = jnp.concatenate([block[:R], block[R:] + edge], axis=0)
                for n, x in enumerate(to_complex(block)):
                    hs[a, n, f * R:f * R + R, b * R:b * R + R] = x
        return carry

    loop(0, 4, tap_spectrum, 0)

    for n in range(2):
        arrived(n)
        for d in range(3):
            pl.when(exists(-pieces[n][0], 0))(passes[d][n].start)

    loop(4, PARTS, tap_spectrum, 0)

    loads[0].wait()
    for n in (2, 3):
        arrived(n)

    def mask_columns(values):
        h_, l_ = split(values)
        return [split(dot3(h_, l_, rh[:, b * T:b * T + T], rl[:, b * T:b * T + T])) for b in range(2)]

    for b, (h_, l_) in enumerate(mask_columns(win[mid, :])):
        mpart[:, b * T:b * T + T] = dot3(th[:, mid], tl[:, mid], h_, l_)

    for n in range(4, 8):
        arrived(n)
    for d in range(1, 4):
        q = lax.rem(j + 4 - d, 4)
        for n, start in enumerate((R + T, 0)):
            at = win.at[quarter(start, q), mid]
            came = remote(at, at, psend.at[2 * d - 2 + n], precv.at[2 * d - 2 + n], {"kern": peer[d]})
            pl.when(exists(-pieces[n][0], 0))(came.wait_recv)

    outer = [jnp.concatenate([t[:, low], t[:, high]], axis=1) for t in (th, tl)]
    for b, (h_, l_) in enumerate(mask_columns(jnp.concatenate([win[low, :], win[high, :]], axis=0))):
        value = mpart[:, b * T:b * T + T] + dot3(*outer, h_, l_)
        for f in range(2):
            for n, x in enumerate(to_complex(value[f * T:f * T + T])):
                ms[n, f * R:f * R + R, b * R:b * R + R] = x

    def inverse_rows(a, carry):
        for b in range(2):
            quads = []
            for f in range(2):
                at = (slice(f * R, f * R + R), slice(b * R, b * R + R))
                m = [ms[n, at[0], at[1]] for n in range(4)]
                h = [hs[a, n, at[0], at[1]] for n in range(4)]
                y = []
                for n in (0, 2):
                    y.append(m[n] * h[n] + m[n + 1] * h[n + 1])
                    y.append(m[n + 1] * h[n] - m[n] * h[n + 1])
                quads.append(from_complex(*y))
            at = slice(b * T, b * T + T)
            h_, l_ = split(dot3(rh[:T, :], rl[:T, :], *spectrum_block(quads)))
            vh[a, :, at] = h_
            vl[a, :, at] = l_
        return carry

    loop(0, PARTS, inverse_rows, 0)

    def partner(kind, at):
        return at + 1 - 2 * lax.rem(at, 2) if kind == 0 else 3 - at

    pair = (partner(0, j), partner(1, j))
    def rows_of(i):
        return slice(i * Q, i * Q + Q)

    def amplitudes(i):
        at = rows_of(i)
        value = dot3(vh[:, at, :].reshape(PARTS * Q, W), vl[:, at, :].reshape(PARTS * Q, W),
                     th[:, :T], tl[:, :T]).reshape(PARTS, Q, T) * SCALE
        amp[:, at, :] = value
        total = None
        for k in range(3):
            term = weights[k] * (value[k] * value[k] + value[k + 3] * value[k + 3])
            total = term if total is None else total + term
        return total

    halves = (slice(0, R), slice(R, T))
    sums = []
    for i in range(4):
        term = amplitudes(i)
        for half in range(2):
            n = 2 * i + half
            ipart[n] = term[:, halves[half]]
            copy = remote(ipart.at[n], ione.at[n], isend.at[n], isem.at[n], {"kern": pair[half]})
            copy.start()
            sums.append(copy)
    shares = []
    for i in range(4):
        for half in range(2):
            n = 2 * i + half
            sums[n].wait_recv()
            imid[n] = ipart[n] + ione[n]
            copy = remote(imid.at[n], itwo.at[n], asend.at[n], asem.at[n], {"kern": pair[1 - half]})
            copy.start()
            shares.append(copy)

    loads[5].wait()
    for i in range(4):
        at = rows_of(i)
        for half in range(2):
            shares[2 * i + half].wait_recv()
        intensity = jnp.concatenate([imid[2 * i] + itwo[2 * i], imid[2 * i + 1] + itwo[2 * i + 1]], axis=1) * (1.0 / 12.0)
        x = 1.0 / (1.0 + jnp.exp(-8.0 * (intensity - 0.25)))
        resist[at, :] = x
        factor = 2.0 * (x - targ[at, :].astype(F32)) * 8.0 * x * (1.0 - x)
        both = [split(factor * (weights[a % 3] * (2.0 / 12.0)) * amp[a, at, :]) for a in range(PARTS)]
        h_ = jnp.concatenate([x[0] for x in both], axis=0)
        l_ = jnp.concatenate([x[1] for x in both], axis=0)
        for b in range(2):
            cut = slice(b * T, b * T + T)
            u, v = split(dot3(h_, l_, rh[:T, cut], rl[:T, cut]).reshape(PARTS, Q, T))
            ph[:, at, cut] = u
            pw[:, at, cut] = v

    firsts = [None] * 8
    for b in range(2):
        at = slice(b * T, b * T + T)

        def gather(a, carry, at=at, b=b):
            value = dot3(th[:, :T], tl[:, :T], ph[a, :, at], pw[a, :, at])
            for f in range(2):
                p = to_complex(value[f * T:f * T + T])
                fr = slice(f * R, f * R + R)
                h = [hs[a, n, fr, b * R:b * R + R] for n in range(4)]
                for n in (0, 2):
                    for m, x in ((n, p[n] * h[n] - p[n + 1] * h[n + 1]), (n + 1, p[n] * h[n + 1] + p[n + 1] * h[n])):
                        acc[m, fr, :] = x if a == 0 else acc[m, fr, :] + x
            return carry

        loop(0, PARTS, gather, 0)
        quads = [from_complex(*[acc[i, f * R:f * R + R, :] for i in range(4)]) for f in range(2)]
        value = dot3(rh[...], rl[...], *spectrum_block(quads))
        for half in range(2):
            for q in range(4):
                for far in range(2):
                    m = (q + 6) % 8 if far == 0 else q + 2
                    tsend[2 * b + half, q, far] = value[m * Q:m * Q + Q, half * R:half * R + R]
        for kind in range(2):
            for half in range(2):
                n = 2 * b + half
                to = pair[half]
                owner = partner(1 - half, to) if kind == 0 else to
                at = 4 * kind + n
                copy = remote(tsend.at[n, owner], tone.at[at], tss.at[at], trs.at[at], {"kern": to})
                copy.start()
                firsts[at] = copy

    seconds = []
    for n in range(4):
        to = pair[1 - n % 2]
        firsts[n].wait_recv()
        tmid[n] = tsend[n, to] + tone[n]
        copy = remote(tmid.at[n], ttwo.at[n], uss.at[n], urs.at[n], {"kern": to})
        copy.start()
        seconds.append(copy)

    pixel_rows = None
    for b in range(2):
        parts = []
        for n in (2 * b, 2 * b + 1):
            firsts[4 + n].wait_recv()
            seconds[n].wait_recv()
            parts.append((tsend[n, j] + tone[4 + n] + ttwo[n]).reshape(2 * Q, R))
        g_h, g_l = split(jnp.concatenate(parts, axis=1))
        term = dot3(g_h, g_l, th[b * T:b * T + T, :], tl[b * T:b * T + T, :])
        pixel_rows = term if b == 0 else pixel_rows + term
    gw[...] = pixel_rows
    far_rows, near_rows = slice(0, Q), slice(Q, 2 * Q)
    west, east = exists(0, -1), exists(0, 1)
    ends = [
        (gives, takes, gw.at[far_rows, mid], ecen, device(step, 0)),
        (jnp.logical_and(gives, west), jnp.logical_and(takes, east), gw.at[far_rows, low], eside.at[0], device(step, -1)),
        (jnp.logical_and(gives, east), jnp.logical_and(takes, west), gw.at[far_rows, high], eside.at[1], device(step, 1)),
        (west, east, gw.at[near_rows, low], eside.at[2], device(0, -1)),
        (east, west, gw.at[near_rows, high], eside.at[3], device(0, 1)),
    ]
    hops = [remote(src, dst, ess.at[n], ers.at[n], to) for n, (_, _, src, dst, to) in enumerate(ends)]
    for n in range(5):
        pl.when(ends[n][0])(hops[n].start)
    lane = lax.broadcasted_iota(jnp.int32, (1, T), 1) // 64
    pixels = jnp.zeros((1, T), F32)
    for k in range(4):
        pixels = jnp.where(lane == k, active[j, k].astype(F32), pixels)
    pixels = pixels * SCALE
    for n in range(5):
        pl.when(ends[n][1])(hops[n].wait_recv)
    own_part = gw[near_rows, mid] + ecen[...]
    gradient[:, :R] = (own_part[:, :R] + eside[1] + eside[3]) * pixels[:, :R]
    gradient[:, R:] = (own_part[:, R:] + eside[0] + eside[2]) * pixels[:, R:]


    for n in range(8):
        pl.when(exists(*pieces[n][:2]))(copies[n].wait_send)
    for n in range(2):
        for d in range(3):
            pl.when(exists(-pieces[n][0], 0))(passes[d][n].wait_send)
    for copy in sums + shares + firsts + seconds:
        copy.wait_send()
    for n in range(5):
        pl.when(ends[n][0])(hops[n].wait_send)


def local(photomask, target_bits, active_blocks, kernel_taps, kernel_weights):
    hbm = pl.BlockSpec(memory_space=pl.ANY)
    smem = pl.BlockSpec(memory_space=pltpu.SMEM)
    vmem = pltpu.VMEM
    dma = pltpu.SemaphoreType.DMA
    scratch = [
        vmem((W, W), F32),
        vmem((2, 3, 2 * R + 1, 2 * R + 1), F32),
        vmem((W, W), BF), vmem((W, W), BF), vmem((W, W), BF), vmem((W, W), BF),
        vmem((T, T), jnp.int32),
        vmem((8, T), F32),
        vmem((8, W), F32),
        vmem((W, W), BF), vmem((W, W), BF),
        vmem((W, W), F32),
        vmem((PARTS, 4, T, T), F32),
        vmem((4, T, T), F32),
        vmem((PARTS, T, W), BF), vmem((PARTS, T, W), BF),
        vmem((PARTS, T, T), F32),
        vmem((PARTS, T, W), BF), vmem((PARTS, T, W), BF),
        vmem((8, Q, R), F32), vmem((8, Q, R), F32), vmem((8, Q, R), F32), vmem((8, Q, R), F32),
        vmem((4, T, R), F32),
        vmem((4, 4, 2, Q, R), F32),
        vmem((8, 2, Q, R), F32), vmem((4, 2, Q, R), F32), vmem((4, 2, Q, R), F32),
        vmem((2 * Q, W), F32),
        vmem((Q, T), F32), vmem((4, Q, R), F32),
        dma((14,)), dma((8,)), dma((8,)),
        dma((6,)), dma((6,)),
        dma((8,)), dma((8,)), dma((8,)), dma((8,)),
        dma((8,)), dma((8,)), dma((4,)), dma((4,)),
        dma((5,)), dma((5,)),
    ]
    return pl.pallas_call(
        kernel,
        out_shape=(vmem((Q, T), F32), vmem((T, T), F32)),
        in_specs=[hbm, hbm, smem, hbm, smem, hbm, hbm, hbm, hbm],
        out_specs=(pl.BlockSpec(memory_space=vmem), pl.BlockSpec(memory_space=vmem)),
        scratch_shapes=scratch,
        compiler_params=pltpu.CompilerParams(
            collective_id=0, has_side_effects=True, vmem_limit_bytes=56 * 1024 * 1024),
        name="socs",
    )(photomask, target_bits, active_blocks, kernel_taps.transpose(1, 2, 0, 3), kernel_weights,
      *[jnp.asarray(t) for t in tables()])


def solution(mesh):
    in_specs = (
        P("row", "col"),
        P("row", "col"),
        P("row", "col"),
        P(None, "kern", None, None),
        P("kern"),
    )
    out_specs = (P(("row", "kern"), "col"), P("row", "col"))
    return jax.shard_map(local, mesh=mesh, in_specs=in_specs, out_specs=out_specs, check_vma=False)
```

```python
import functools

import jax
import jax.numpy as jnp
import numpy as np
from jax import lax
from jax.experimental import pallas as pl
from jax.experimental.pallas import tpu as pltpu
from jax.sharding import PartitionSpec as P

MESH = pl.DeviceIdType.MESH
T = 256
W = 512
R = 128
PARTS = 6
Q = 64
SCALE = 2.0 ** -17
F32 = jnp.float32
BF = jnp.bfloat16


def tables():
    sample = np.arange(W)[:, None]
    freq = np.arange(T)[None, :]
    angle = np.pi / W * (sample * (2 * freq + 1) % (2 * W))
    cos, sin = np.cos(angle), np.sin(angle)
    full = np.concatenate([cos[:, :R], sin[:, :R], cos[:, R:], sin[:, R:]], axis=1)
    full[np.abs(full) < 1e-12] = 0.0
    high = full.astype(BF)
    low = (full - high.astype(np.float64)).astype(BF)
    return high, low, np.ascontiguousarray(high.T), np.ascontiguousarray(low.T)


def split(value):
    high = value.astype(BF)
    return high, (value - high.astype(F32)).astype(BF)


def dot(a, b):
    return jnp.dot(a, b, preferred_element_type=F32)


def dot3(ah, al, bh, bl):
    return dot(ah, bh) + dot(al, bh) + dot(ah, bl)


def to_complex(block):
    cc, cs = block[:R, :R], block[:R, R:]
    sc, ss = block[R:, :R], block[R:, R:]
    return cc - ss, -(cs + sc), cc + ss, cs - sc


def from_complex(pr, pi, mr, mi):
    return pr + mr, mi - pi, -(pi + mi), mr - pr


def loop(lo, hi, fn, init):
    for i in range(lo, hi):
        fn(i, init)


def spectrum_block(quads):
    rows = []
    for cc, cs, sc, ss in quads:
        rows += [jnp.concatenate([cc, cs], axis=1), jnp.concatenate([sc, ss], axis=1)]
    return split(jnp.concatenate(rows, axis=0))


def kernel(
    mask, target, active, taps, weights, rh_in, rl_in, th_in, tl_in,
    gradient, resist,
    win, tapv, rh, rl, th, tl, targ, taph, rhat, xh, xl, mpart, hs, ms, vh, vl, amp, ph, pw,
    ipart, ione, imid, itwo, acc, tsend, tone, tmid, ttwo, gw, ecen, eside,
    lsem, msend, mrecv, psend, precv, isend, isem, asend, asem, tss, trs, uss, urs, ess, ers,
):
    r, c, j = lax.axis_index("row"), lax.axis_index("col"), lax.axis_index("kern")
    rows, cols = lax.axis_size("row"), lax.axis_size("col")
    def exists(dr, dc):
        ok = None
        for at, d, n in ((r, dr, rows), (c, dc, cols)):
            if d:
                one = at > 0 if d < 0 else at < n - 1
                ok = one if ok is None else jnp.logical_and(ok, one)
        return ok

    def device(dr, dc):
        return {"row": r + dr, "col": c + dc}

    around = [(dr, dc) for dr in (-1, 0, 1) for dc in (-1, 0, 1) if dr or dc]
    down = j < 2
    step = jnp.where(down, 1, -1)
    gives = jnp.logical_or(jnp.logical_and(down, r < rows - 1), jnp.logical_and(jnp.logical_not(down), r > 0))
    takes = jnp.logical_or(jnp.logical_and(down, r > 0), jnp.logical_and(jnp.logical_not(down), r < rows - 1))
    peer = [lax.rem(j + d, 4) for d in range(4)]

    ecen[...] = jnp.zeros_like(ecen)
    eside[...] = jnp.zeros_like(eside)
    barrier = pltpu.get_barrier_semaphore()
    count = 3
    for dr, dc in around:
        ok = exists(dr, dc)
        count = count + ok.astype(jnp.int32)

        @pl.when(ok)
        def _(dr=dr, dc=dc):
            pl.semaphore_signal(barrier, inc=1, device_id=device(dr, dc), device_id_type=MESH)
    for d in range(1, 4):
        pl.semaphore_signal(barrier, inc=1, device_id={"kern": peer[d]}, device_id_type=MESH)
    loads = [
        pltpu.make_async_copy(mask, win.at[R:R + T, R:R + T], lsem.at[0]),
        pltpu.make_async_copy(rh_in, rh, lsem.at[1]),
        pltpu.make_async_copy(rl_in, rl, lsem.at[2]),
        pltpu.make_async_copy(th_in, th, lsem.at[3]),
        pltpu.make_async_copy(tl_in, tl, lsem.at[4]),
        pltpu.make_async_copy(target, targ, lsem.at[5]),
    ]
    loads += [
        pltpu.make_async_copy(taps.at[a % 3, :, a // 3, :], tapv.at[a // 3, a % 3], lsem.at[8 + a])
        for a in range(PARTS)
    ]
    for load in loads:
        load.start()

    @pl.when(r == 0)
    def _():
        win[:R, :] = jnp.zeros((R, W), F32)

    @pl.when(r == rows - 1)
    def _():
        win[R + T:, :] = jnp.zeros((R, W), F32)

    @pl.when(c == 0)
    def _():
        win[:, :R] = jnp.zeros((W, R), F32)

    @pl.when(c == cols - 1)
    def _():
        win[:, R + T:] = jnp.zeros((W, R), F32)

    pl.semaphore_wait(barrier, count)

    def remote(src, dst, s, d, to):
        return pltpu.make_async_remote_copy(
            src_ref=src, dst_ref=dst, send_sem=s, recv_sem=d, device_id=to, device_id_type=MESH)

    low, mid, high = slice(0, R), slice(R, R + T), slice(R + T, W)
    part_rows = R // 4

    def quarter(start, q):
        return pl.ds(pl.multiple_of(start + q * part_rows, part_rows), part_rows)

    pieces = [
        (-1, 0, mask.at[quarter(0, j), :], win.at[quarter(R + T, j), mid]),
        (1, 0, mask.at[quarter(R, j), :], win.at[quarter(0, j), mid]),
        (0, -1, mask.at[:, 0:R], win.at[mid, high]),
        (0, 1, mask.at[:, R:T], win.at[mid, low]),
        (-1, -1, mask.at[0:R, 0:R], win.at[high, high]),
        (-1, 1, mask.at[0:R, R:T], win.at[high, low]),
        (1, -1, mask.at[R:T, 0:R], win.at[low, high]),
        (1, 1, mask.at[R:T, R:T], win.at[low, low]),
    ]
    copies = [remote(src, dst, msend.at[n], mrecv.at[n], device(dr, dc))
              for n, (dr, dc, src, dst) in enumerate(pieces)]
    for n in range(4):
        pl.when(exists(*pieces[n][:2]))(copies[n].start)

    def arrived(n):
        pl.when(exists(-pieces[n][0], -pieces[n][1]))(copies[n].wait_recv)

    def passed(d):
        return [
            remote(win.at[quarter(start, j), mid], win.at[quarter(start, j), mid],
                   psend.at[2 * d - 2 + n], precv.at[2 * d - 2 + n], {"kern": peer[d]})
            for n, start in enumerate((R + T, 0))
        ]

    passes = [passed(d) for d in range(1, 4)]

    for load in loads[1:5] + loads[6:]:
        load.wait()
    sign_row = (1 - 2 * (lax.broadcasted_iota(jnp.int32, (1, R), 1) & 1)).astype(F32)
    sign_col = (1 - 2 * (lax.broadcasted_iota(jnp.int32, (R, 1), 0) & 1)).astype(F32)
    taph[...] = jnp.zeros_like(taph)
    for a in range(PARTS):
        taph[a:a + 1, :] = tapv[a // 3, a % 3, T:T + 1, 0:T]
    edge_h, edge_l = split(taph[...])
    rhat[...] = dot3(edge_h, edge_l, rh[:T, :], rl[:T, :])
    for a in range(PARTS):
        corner = tapv[a // 3, a % 3, T:T + 1, T:T + 1]
        for b in range(2):
            at = slice(b * T + R, b * T + T)
            rhat[a:a + 1, at] = rhat[a:a + 1, at] + corner * sign_row

    def tap_spectrum(a, carry):
        part, k = a // 3, a % 3
        low_h, low_l = split(tapv[part, k, 0:T, 0:T])
        column = tapv[part, k, 0:T, T:T + 1]
        for b in range(2):
            at = slice(b * T, b * T + T)
            value = dot3(low_h, low_l, rh[:T, at], rl[:T, at])
            value = jnp.concatenate([value[:, :R], value[:, R:] + column * sign_row], axis=1)
            vh_, vl_ = split(value)
            xh[:T, at] = vh_
            xl[:T, at] = vl_
        for b in range(2):
            at = slice(b * T, b * T + T)
            value = dot3(th[:, :T], tl[:, :T], xh[:T, at], xl[:T, at])
            edge = sign_col * rhat[a:a + 1, at]
            for f in range(2):
                block = value[f * T:f * T + T]
                block = jnp.concatenate([block[:R], block[R:] + edge], axis=0)
                for n, x in enumerate(to_complex(block)):
                    hs[a, n, f * R:f * R + R, b * R:b * R + R] = x
        return carry

    for n in range(4, 8):
        pl.when(exists(*pieces[n][:2]))(copies[n].start)
    loop(0, 2, tap_spectrum, 0)

    for n in range(2):
        arrived(n)
        for d in range(3):
            pl.when(exists(-pieces[n][0], 0))(passes[d][n].start)

    loop(2, PARTS, tap_spectrum, 0)

    loads[0].wait()
    for n in (2, 3):
        arrived(n)

    def mask_columns(values):
        h_, l_ = split(values)
        return [split(dot3(h_, l_, rh[:, b * T:b * T + T], rl[:, b * T:b * T + T])) for b in range(2)]

    for b, (h_, l_) in enumerate(mask_columns(win[mid, :])):
        mpart[:, b * T:b * T + T] = dot3(th[:, mid], tl[:, mid], h_, l_)

    for n in range(4, 8):
        arrived(n)
    for d in range(1, 4):
        q = lax.rem(j + 4 - d, 4)
        for n, start in enumerate((R + T, 0)):
            at = win.at[quarter(start, q), mid]
            came = remote(at, at, psend.at[2 * d - 2 + n], precv.at[2 * d - 2 + n], {"kern": peer[d]})
            pl.when(exists(-pieces[n][0], 0))(came.wait_recv)

    outer = [jnp.concatenate([t[:, low], t[:, high]], axis=1) for t in (th, tl)]
    for b, (h_, l_) in enumerate(mask_columns(jnp.concatenate([win[low, :], win[high, :]], axis=0))):
        value = mpart[:, b * T:b * T + T] + dot3(*outer, h_, l_)
        for f in range(2):
            for n, x in enumerate(to_complex(value[f * T:f * T + T])):
                ms[n, f * R:f * R + R, b * R:b * R + R] = x

    def inverse_rows(a, carry):
        for b in range(2):
            quads = []
            for f in range(2):
                at = (slice(f * R, f * R + R), slice(b * R, b * R + R))
                m = [ms[n, at[0], at[1]] for n in range(4)]
                h = [hs[a, n, at[0], at[1]] for n in range(4)]
                y = []
                for n in (0, 2):
                    y.append(m[n] * h[n] + m[n + 1] * h[n + 1])
                    y.append(m[n + 1] * h[n] - m[n] * h[n + 1])
                quads.append(from_complex(*y))
            at = slice(b * T, b * T + T)
            h_, l_ = split(dot3(rh[:T, :], rl[:T, :], *spectrum_block(quads)))
            vh[a, :, at] = h_
            vl[a, :, at] = l_
        return carry

    loop(0, PARTS, inverse_rows, 0)

    def partner(kind, at):
        return at + 1 - 2 * lax.rem(at, 2) if kind == 0 else 3 - at

    pair = (partner(0, j), partner(1, j))
    def rows_of(i):
        return slice(i * Q, i * Q + Q)

    def amplitudes(i):
        at = rows_of(i)
        value = dot3(vh[:, at, :].reshape(PARTS * Q, W), vl[:, at, :].reshape(PARTS * Q, W),
                     th[:, :T], tl[:, :T]).reshape(PARTS, Q, T) * SCALE
        amp[:, at, :] = value
        total = None
        for k in range(3):
            term = weights[k] * (value[k] * value[k] + value[k + 3] * value[k + 3])
            total = term if total is None else total + term
        return total

    halves = (slice(0, R), slice(R, T))
    sums = []
    for i in range(4):
        term = amplitudes(i)
        for half in range(2):
            n = 2 * i + half
            ipart[n] = term[:, halves[half]]
            copy = remote(ipart.at[n], ione.at[n], isend.at[n], isem.at[n], {"kern": pair[half]})
            copy.start()
            sums.append(copy)
    shares = []
    for i in range(4):
        for half in range(2):
            n = 2 * i + half
            sums[n].wait_recv()
            imid[n] = ipart[n] + ione[n]
            copy = remote(imid.at[n], itwo.at[n], asend.at[n], asem.at[n], {"kern": pair[1 - half]})
            copy.start()
            shares.append(copy)

    loads[5].wait()
    for i in range(4):
        at = rows_of(i)
        for half in range(2):
            shares[2 * i + half].wait_recv()
        intensity = jnp.concatenate([imid[2 * i] + itwo[2 * i], imid[2 * i + 1] + itwo[2 * i + 1]], axis=1) * (1.0 / 12.0)
        x = 1.0 / (1.0 + jnp.exp(-8.0 * (intensity - 0.25)))
        resist[at, :] = x
        factor = 2.0 * (x - targ[at, :].astype(F32)) * 8.0 * x * (1.0 - x)
        both = [split(factor * (weights[a % 3] * (2.0 / 12.0)) * amp[a, at, :]) for a in range(PARTS)]
        h_ = jnp.concatenate([x[0] for x in both], axis=0)
        l_ = jnp.concatenate([x[1] for x in both], axis=0)
        for b in range(2):
            cut = slice(b * T, b * T + T)
            u, v = split(dot3(h_, l_, rh[:T, cut], rl[:T, cut]).reshape(PARTS, Q, T))
            ph[:, at, cut] = u
            pw[:, at, cut] = v

    firsts = [None] * 8
    for b in range(2):
        at = slice(b * T, b * T + T)

        def gather(a, carry, at=at, b=b):
            value = dot3(th[:, :T], tl[:, :T], ph[a, :, at], pw[a, :, at])
            for f in range(2):
                p = to_complex(value[f * T:f * T + T])
                fr = slice(f * R, f * R + R)
                h = [hs[a, n, fr, b * R:b * R + R] for n in range(4)]
                for n in (0, 2):
                    for m, x in ((n, p[n] * h[n] - p[n + 1] * h[n + 1]), (n + 1, p[n] * h[n + 1] + p[n + 1] * h[n])):
                        acc[m, fr, :] = x if a == 0 else acc[m, fr, :] + x
            return carry

        loop(0, PARTS, gather, 0)
        quads = [from_complex(*[acc[i, f * R:f * R + R, :] for i in range(4)]) for f in range(2)]
        value = dot3(rh[...], rl[...], *spectrum_block(quads))
        for half in range(2):
            for q in range(4):
                for far in range(2):
                    m = (q + 6) % 8 if far == 0 else q + 2
                    tsend[2 * b + half, q, far] = value[m * Q:m * Q + Q, half * R:half * R + R]
        for kind in range(2):
            for half in range(2):
                n = 2 * b + half
                to = pair[half]
                owner = partner(1 - half, to) if kind == 0 else to
                at = 4 * kind + n
                copy = remote(tsend.at[n, owner], tone.at[at], tss.at[at], trs.at[at], {"kern": to})
                copy.start()
                firsts[at] = copy

    seconds = []
    for n in range(4):
        to = pair[1 - n % 2]
        firsts[n].wait_recv()
        tmid[n] = tsend[n, to] + tone[n]
        copy = remote(tmid.at[n], ttwo.at[n], uss.at[n], urs.at[n], {"kern": to})
        copy.start()
        seconds.append(copy)

    pixel_rows = None
    for b in range(2):
        parts = []
        for n in (2 * b, 2 * b + 1):
            firsts[4 + n].wait_recv()
            seconds[n].wait_recv()
            parts.append((tsend[n, j] + tone[4 + n] + ttwo[n]).reshape(2 * Q, R))
        g_h, g_l = split(jnp.concatenate(parts, axis=1))
        term = dot3(g_h, g_l, th[b * T:b * T + T, :], tl[b * T:b * T + T, :])
        pixel_rows = term if b == 0 else pixel_rows + term
    gw[...] = pixel_rows
    far_rows, near_rows = slice(0, Q), slice(Q, 2 * Q)
    west, east = exists(0, -1), exists(0, 1)
    ends = [
        (gives, takes, gw.at[far_rows, mid], ecen, device(step, 0)),
        (jnp.logical_and(gives, west), jnp.logical_and(takes, east), gw.at[far_rows, low], eside.at[0], device(step, -1)),
        (jnp.logical_and(gives, east), jnp.logical_and(takes, west), gw.at[far_rows, high], eside.at[1], device(step, 1)),
        (west, east, gw.at[near_rows, low], eside.at[2], device(0, -1)),
        (east, west, gw.at[near_rows, high], eside.at[3], device(0, 1)),
    ]
    hops = [remote(src, dst, ess.at[n], ers.at[n], to) for n, (_, _, src, dst, to) in enumerate(ends)]
    for n in range(5):
        pl.when(ends[n][0])(hops[n].start)
    lane = lax.broadcasted_iota(jnp.int32, (1, T), 1) // 64
    pixels = jnp.zeros((1, T), F32)
    for k in range(4):
        pixels = jnp.where(lane == k, active[j, k].astype(F32), pixels)
    pixels = pixels * SCALE
    for n in range(5):
        pl.when(ends[n][1])(hops[n].wait_recv)
    own_part = gw[near_rows, mid] + ecen[...]
    gradient[:, :R] = (own_part[:, :R] + eside[1] + eside[3]) * pixels[:, :R]
    gradient[:, R:] = (own_part[:, R:] + eside[0] + eside[2]) * pixels[:, R:]


    for n in range(8):
        pl.when(exists(*pieces[n][:2]))(copies[n].wait_send)
    for n in range(2):
        for d in range(3):
            pl.when(exists(-pieces[n][0], 0))(passes[d][n].wait_send)
    for copy in sums + shares + firsts + seconds:
        copy.wait_send()
    for n in range(5):
        pl.when(ends[n][0])(hops[n].wait_send)


def local(photomask, target_bits, active_blocks, kernel_taps, kernel_weights):
    hbm = pl.BlockSpec(memory_space=pl.ANY)
    smem = pl.BlockSpec(memory_space=pltpu.SMEM)
    vmem = pltpu.VMEM
    dma = pltpu.SemaphoreType.DMA
    scratch = [
        vmem((W, W), F32),
        vmem((2, 3, 2 * R + 1, 2 * R + 1), F32),
        vmem((W, W), BF), vmem((W, W), BF), vmem((W, W), BF), vmem((W, W), BF),
        vmem((T, T), jnp.int32),
        vmem((8, T), F32),
        vmem((8, W), F32),
        vmem((W, W), BF), vmem((W, W), BF),
        vmem((W, W), F32),
        vmem((PARTS, 4, T, T), F32),
        vmem((4, T, T), F32),
        vmem((PARTS, T, W), BF), vmem((PARTS, T, W), BF),
        vmem((PARTS, T, T), F32),
        vmem((PARTS, T, W), BF), vmem((PARTS, T, W), BF),
        vmem((8, Q, R), F32), vmem((8, Q, R), F32), vmem((8, Q, R), F32), vmem((8, Q, R), F32),
        vmem((4, T, R), F32),
        vmem((4, 4, 2, Q, R), F32),
        vmem((8, 2, Q, R), F32), vmem((4, 2, Q, R), F32), vmem((4, 2, Q, R), F32),
        vmem((2 * Q, W), F32),
        vmem((Q, T), F32), vmem((4, Q, R), F32),
        dma((14,)), dma((8,)), dma((8,)),
        dma((6,)), dma((6,)),
        dma((8,)), dma((8,)), dma((8,)), dma((8,)),
        dma((8,)), dma((8,)), dma((4,)), dma((4,)),
        dma((5,)), dma((5,)),
    ]
    return pl.pallas_call(
        kernel,
        out_shape=(vmem((Q, T), F32), vmem((T, T), F32)),
        in_specs=[hbm, hbm, smem, hbm, smem, hbm, hbm, hbm, hbm],
        out_specs=(pl.BlockSpec(memory_space=vmem), pl.BlockSpec(memory_space=vmem)),
        scratch_shapes=scratch,
        compiler_params=pltpu.CompilerParams(
            collective_id=0, has_side_effects=True, vmem_limit_bytes=56 * 1024 * 1024),
        name="socs",
    )(photomask, target_bits, active_blocks, kernel_taps.transpose(1, 2, 0, 3), kernel_weights,
      *[jnp.asarray(t) for t in tables()])


def solution(mesh):
    in_specs = (
        P("row", "col"),
        P("row", "col"),
        P("row", "col"),
        P(None, "kern", None, None),
        P("kern"),
    )
    out_specs = (P(("row", "kern"), "col"), P("row", "col"))
    return jax.shard_map(local, mesh=mesh, in_specs=in_specs, out_specs=out_specs, check_vma=False)
```

```python
import functools

import jax
import jax.numpy as jnp
import numpy as np
from jax import lax
from jax.experimental import pallas as pl
from jax.experimental.pallas import tpu as pltpu
from jax.sharding import PartitionSpec as P

MESH = pl.DeviceIdType.MESH
T = 256
W = 512
R = 128
PARTS = 6
Q = 64
SCALE = 2.0 ** -17
F32 = jnp.float32
BF = jnp.bfloat16


def tables():
    sample = np.arange(W)[:, None]
    freq = np.arange(T)[None, :]
    angle = np.pi / W * (sample * (2 * freq + 1) % (2 * W))
    cos, sin = np.cos(angle), np.sin(angle)
    full = np.concatenate([cos[:, :R], sin[:, :R], cos[:, R:], sin[:, R:]], axis=1)
    full[np.abs(full) < 1e-12] = 0.0
    high = full.astype(BF)
    low = (full - high.astype(np.float64)).astype(BF)
    return high, low, np.ascontiguousarray(high.T), np.ascontiguousarray(low.T)


def split(value):
    high = value.astype(BF)
    return high, (value - high.astype(F32)).astype(BF)


def dot(a, b):
    return jnp.dot(a, b, preferred_element_type=F32)


def dot3(ah, al, bh, bl):
    return dot(ah, bh) + dot(al, bh) + dot(ah, bl)


def to_complex(block):
    cc, cs = block[:R, :R], block[:R, R:]
    sc, ss = block[R:, :R], block[R:, R:]
    return cc - ss, -(cs + sc), cc + ss, cs - sc


def from_complex(pr, pi, mr, mi):
    return pr + mr, mi - pi, -(pi + mi), mr - pr


def loop(lo, hi, fn, init):
    for i in range(lo, hi):
        fn(i, init)


def spectrum_block(quads):
    rows = []
    for cc, cs, sc, ss in quads:
        rows += [jnp.concatenate([cc, cs], axis=1), jnp.concatenate([sc, ss], axis=1)]
    return split(jnp.concatenate(rows, axis=0))


def kernel(
    mask, target, active, taps, weights, rh_in, rl_in, th_in, tl_in,
    gradient, resist,
    win, tapv, rh, rl, th, tl, targ, taph, rhat, xh, xl, mpart, hs, ms, vh, vl, amp, ph, pw,
    ipart, ione, imid, itwo, acc, tsend, tone, tmid, ttwo, gw, ecen, eside,
    lsem, msend, mrecv, psend, precv, isend, isem, asend, asem, tss, trs, uss, urs, ess, ers,
):
    r, c, j = lax.axis_index("row"), lax.axis_index("col"), lax.axis_index("kern")
    rows, cols = lax.axis_size("row"), lax.axis_size("col")
    def exists(dr, dc):
        ok = None
        for at, d, n in ((r, dr, rows), (c, dc, cols)):
            if d:
                one = at > 0 if d < 0 else at < n - 1
                ok = one if ok is None else jnp.logical_and(ok, one)
        return ok

    def device(dr, dc):
        return {"row": r + dr, "col": c + dc}

    around = [(dr, dc) for dr in (-1, 0, 1) for dc in (-1, 0, 1) if dr or dc]
    down = j < 2
    step = jnp.where(down, 1, -1)
    gives = jnp.logical_or(jnp.logical_and(down, r < rows - 1), jnp.logical_and(jnp.logical_not(down), r > 0))
    takes = jnp.logical_or(jnp.logical_and(down, r > 0), jnp.logical_and(jnp.logical_not(down), r < rows - 1))
    peer = [lax.rem(j + d, 4) for d in range(4)]

    ecen[...] = jnp.zeros_like(ecen)
    eside[...] = jnp.zeros_like(eside)
    barrier = pltpu.get_barrier_semaphore()
    count = 3
    for dr, dc in around:
        ok = exists(dr, dc)
        count = count + ok.astype(jnp.int32)

        @pl.when(ok)
        def _(dr=dr, dc=dc):
            pl.semaphore_signal(barrier, inc=1, device_id=device(dr, dc), device_id_type=MESH)
    for d in range(1, 4):
        pl.semaphore_signal(barrier, inc=1, device_id={"kern": peer[d]}, device_id_type=MESH)
    loads = [
        pltpu.make_async_copy(mask, win.at[R:R + T, R:R + T], lsem.at[0]),
        pltpu.make_async_copy(rh_in, rh, lsem.at[1]),
        pltpu.make_async_copy(rl_in, rl, lsem.at[2]),
        pltpu.make_async_copy(th_in, th, lsem.at[3]),
        pltpu.make_async_copy(tl_in, tl, lsem.at[4]),
        pltpu.make_async_copy(target, targ, lsem.at[5]),
    ]
    loads += [
        pltpu.make_async_copy(taps.at[a % 3, :, a // 3, :], tapv.at[a // 3, a % 3], lsem.at[8 + a])
        for a in range(PARTS)
    ]
    for load in loads:
        load.start()

    @pl.when(r == 0)
    def _():
        win[:R, :] = jnp.zeros((R, W), F32)

    @pl.when(r == rows - 1)
    def _():
        win[R + T:, :] = jnp.zeros((R, W), F32)

    @pl.when(c == 0)
    def _():
        win[:, :R] = jnp.zeros((W, R), F32)

    @pl.when(c == cols - 1)
    def _():
        win[:, R + T:] = jnp.zeros((W, R), F32)

    pl.semaphore_wait(barrier, count)

    def remote(src, dst, s, d, to):
        return pltpu.make_async_remote_copy(
            src_ref=src, dst_ref=dst, send_sem=s, recv_sem=d, device_id=to, device_id_type=MESH)

    low, mid, high = slice(0, R), slice(R, R + T), slice(R + T, W)
    part_rows = R // 4

    def quarter(start, q):
        return pl.ds(pl.multiple_of(start + q * part_rows, part_rows), part_rows)

    pieces = [
        (-1, 0, mask.at[quarter(0, j), :], win.at[quarter(R + T, j), mid]),
        (1, 0, mask.at[quarter(R, j), :], win.at[quarter(0, j), mid]),
        (0, -1, mask.at[:, 0:R], win.at[mid, high]),
        (0, 1, mask.at[:, R:T], win.at[mid, low]),
        (-1, -1, mask.at[0:R, 0:R], win.at[high, high]),
        (-1, 1, mask.at[0:R, R:T], win.at[high, low]),
        (1, -1, mask.at[R:T, 0:R], win.at[low, high]),
        (1, 1, mask.at[R:T, R:T], win.at[low, low]),
    ]
    copies = [remote(src, dst, msend.at[n], mrecv.at[n], device(dr, dc))
              for n, (dr, dc, src, dst) in enumerate(pieces)]
    for n in range(8):
        pl.when(exists(*pieces[n][:2]))(copies[n].start)

    def arrived(n):
        pl.when(exists(-pieces[n][0], -pieces[n][1]))(copies[n].wait_recv)

    def passed(d):
        return [
            remote(win.at[quarter(start, j), mid], win.at[quarter(start, j), mid],
                   psend.at[2 * d - 2 + n], precv.at[2 * d - 2 + n], {"kern": peer[d]})
            for n, start in enumerate((R + T, 0))
        ]

    passes = [passed(d) for d in range(1, 4)]

    for load in loads[1:5] + loads[6:]:
        load.wait()
    sign_row = (1 - 2 * (lax.broadcasted_iota(jnp.int32, (1, R), 1) & 1)).astype(F32)
    sign_col = (1 - 2 * (lax.broadcasted_iota(jnp.int32, (R, 1), 0) & 1)).astype(F32)
    taph[...] = jnp.zeros_like(taph)
    for a in range(PARTS):
        taph[a:a + 1, :] = tapv[a // 3, a % 3, T:T + 1, 0:T]
    edge_h, edge_l = split(taph[...])
    rhat[...] = dot3(edge_h, edge_l, rh[:T, :], rl[:T, :])
    for a in range(PARTS):
        corner = tapv[a // 3, a % 3, T:T + 1, T:T + 1]
        for b in range(2):
            at = slice(b * T + R, b * T + T)
            rhat[a:a + 1, at] = rhat[a:a + 1, at] + corner * sign_row

    def tap_spectrum(a, carry):
        part, k = a // 3, a % 3
        low_h, low_l = split(tapv[part, k, 0:T, 0:T])
        column = tapv[part, k, 0:T, T:T + 1]
        for b in range(2):
            at = slice(b * T, b * T + T)
            value = dot3(low_h, low_l, rh[:T, at], rl[:T, at])
            value = jnp.concatenate([value[:, :R], value[:, R:] + column * sign_row], axis=1)
            vh_, vl_ = split(value)
            xh[:T, at] = vh_
            xl[:T, at] = vl_
        for b in range(2):
            at = slice(b * T, b * T + T)
            value = dot3(th[:, :T], tl[:, :T], xh[:T, at], xl[:T, at])
            edge = sign_col * rhat[a:a + 1, at]
            for f in range(2):
                block = value[f * T:f * T + T]
                block = jnp.concatenate([block[:R], block[R:] + edge], axis=0)
                for n, x in enumerate(to_complex(block)):
                    hs[a, n, f * R:f * R + R, b * R:b * R + R] = x
        return carry

    loop(0, 4, tap_spectrum, 0)

    for n in range(2):
        arrived(n)
        for d in range(3):
            pl.when(exists(-pieces[n][0], 0))(passes[d][n].start)

    loop(4, PARTS, tap_spectrum, 0)

    loads[0].wait()
    for n in (2, 3):
        arrived(n)

    def mask_columns(values):
        h_, l_ = split(values)
        return [split(dot3(h_, l_, rh[:, b * T:b * T + T], rl[:, b * T:b * T + T])) for b in range(2)]

    for b, (h_, l_) in enumerate(mask_columns(win[mid, :])):
        mpart[:, b * T:b * T + T] = dot3(th[:, mid], tl[:, mid], h_, l_)

    for n in range(4, 8):
        arrived(n)
    for d in range(1, 4):
        q = lax.rem(j + 4 - d, 4)
        for n, start in enumerate((R + T, 0)):
            at = win.at[quarter(start, q), mid]
            came = remote(at, at, psend.at[2 * d - 2 + n], precv.at[2 * d - 2 + n], {"kern": peer[d]})
            pl.when(exists(-pieces[n][0], 0))(came.wait_recv)

    outer = [jnp.concatenate([t[:, low], t[:, high]], axis=1) for t in (th, tl)]
    for b, (h_, l_) in enumerate(mask_columns(jnp.concatenate([win[low, :], win[high, :]], axis=0))):
        value = mpart[:, b * T:b * T + T] + dot3(*outer, h_, l_)
        for f in range(2):
            for n, x in enumerate(to_complex(value[f * T:f * T + T])):
                ms[n, f * R:f * R + R, b * R:b * R + R] = x

    def inverse_rows(a, carry):
        for b in range(2):
            quads = []
            for f in range(2):
                at = (slice(f * R, f * R + R), slice(b * R, b * R + R))
                m = [ms[n, at[0], at[1]] for n in range(4)]
                h = [hs[a, n, at[0], at[1]] for n in range(4)]
                y = []
                for n in (0, 2):
                    y.append(m[n] * h[n] + m[n + 1] * h[n + 1])
                    y.append(m[n + 1] * h[n] - m[n] * h[n + 1])
                quads.append(from_complex(*y))
            at = slice(b * T, b * T + T)
            h_, l_ = split(dot3(rh[:T, :], rl[:T, :], *spectrum_block(quads)))
            vh[a, :, at] = h_
            vl[a, :, at] = l_
        return carry

    loop(0, PARTS, inverse_rows, 0)

    def partner(kind, at):
        return at + 1 - 2 * lax.rem(at, 2) if kind == 0 else 3 - at

    pair = (partner(0, j), partner(1, j))
    def rows_of(i):
        return slice(i * Q, i * Q + Q)

    def amplitudes(i):
        at = rows_of(i)
        value = dot3(vh[:, at, :].reshape(PARTS * Q, W), vl[:, at, :].reshape(PARTS * Q, W),
                     th[:, :T], tl[:, :T]).reshape(PARTS, Q, T) * SCALE
        amp[:, at, :] = value
        total = None
        for k in range(3):
            term = weights[k] * (value[k] * value[k] + value[k + 3] * value[k + 3])
            total = term if total is None else total + term
        return total

    halves = (slice(0, R), slice(R, T))
    sums = []
    for i in range(4):
        term = amplitudes(i)
        for half in range(2):
            n = 2 * i + half
            ipart[n] = term[:, halves[half]]
            copy = remote(ipart.at[n], ione.at[n], isend.at[n], isem.at[n], {"kern": pair[half]})
            copy.start()
            sums.append(copy)
    shares = []
    for i in range(4):
        for half in range(2):
            n = 2 * i + half
            sums[n].wait_recv()
            imid[n] = ipart[n] + ione[n]
            copy = remote(imid.at[n], itwo.at[n], asend.at[n], asem.at[n], {"kern": pair[1 - half]})
            copy.start()
            shares.append(copy)

    loads[5].wait()
    for i in range(4):
        at = rows_of(i)
        for half in range(2):
            shares[2 * i + half].wait_recv()
        intensity = jnp.concatenate([imid[2 * i] + itwo[2 * i], imid[2 * i + 1] + itwo[2 * i + 1]], axis=1) * (1.0 / 12.0)
        x = 1.0 / (1.0 + jnp.exp(-8.0 * (intensity - 0.25)))
        resist[at, :] = x
        factor = 2.0 * (x - targ[at, :].astype(F32)) * 8.0 * x * (1.0 - x)
        both = [split(factor * (weights[a % 3] * (2.0 / 12.0)) * amp[a, at, :]) for a in range(PARTS)]
        h_ = jnp.concatenate([x[0] for x in both], axis=0)
        l_ = jnp.concatenate([x[1] for x in both], axis=0)
        for b in range(2):
            cut = slice(b * T, b * T + T)
            u, v = split(dot3(h_, l_, rh[:T, cut], rl[:T, cut]).reshape(PARTS, Q, T))
            ph[:, at, cut] = u
            pw[:, at, cut] = v

    firsts = [None] * 8
    for b in range(2):
        at = slice(b * T, b * T + T)

        def gather(a, carry, at=at, b=b):
            value = dot3(th[:, :T], tl[:, :T], ph[a, :, at], pw[a, :, at])
            for f in range(2):
                p = to_complex(value[f * T:f * T + T])
                fr = slice(f * R, f * R + R)
                h = [hs[a, n, fr, b * R:b * R + R] for n in range(4)]
                for n in (0, 2):
                    for m, x in ((n, p[n] * h[n] - p[n + 1] * h[n + 1]), (n + 1, p[n] * h[n + 1] + p[n + 1] * h[n])):
                        acc[m, fr, :] = x if a == 0 else acc[m, fr, :] + x
            return carry

        loop(0, PARTS, gather, 0)
        quads = [from_complex(*[acc[i, f * R:f * R + R, :] for i in range(4)]) for f in range(2)]
        value = dot3(rh[...], rl[...], *spectrum_block(quads))
        for half in range(2):
            for q in range(4):
                for far in range(2):
                    m = (q + 6) % 8 if far == 0 else q + 2
                    tsend[2 * b + half, q, far] = value[m * Q:m * Q + Q, half * R:half * R + R]
        for kind in range(2):
            for half in range(2):
                n = 2 * b + half
                to = pair[half]
                owner = partner(1 - half, to) if kind == 0 else to
                at = 4 * kind + n
                copy = remote(tsend.at[n, owner], tone.at[at], tss.at[at], trs.at[at], {"kern": to})
                copy.start()
                firsts[at] = copy

    seconds = []
    for n in range(4):
        to = pair[1 - n % 2]
        firsts[n].wait_recv()
        tmid[n] = tsend[n, to] + tone[n]
        copy = remote(tmid.at[n], ttwo.at[n], uss.at[n], urs.at[n], {"kern": to})
        copy.start()
        seconds.append(copy)

    pixel_rows = None
    for b in range(2):
        parts = []
        for n in (2 * b, 2 * b + 1):
            firsts[4 + n].wait_recv()
            seconds[n].wait_recv()
            parts.append((tsend[n, j] + tone[4 + n] + ttwo[n]).reshape(2 * Q, R))
        g_h, g_l = split(jnp.concatenate(parts, axis=1))
        if b == 0:
            pixel_rows = dot3(g_h, g_l, th[:T, :], tl[:T, :])
    far_rows, near_rows = slice(0, Q), slice(Q, 2 * Q)

    def last_block(at):
        gw[at, :] = pixel_rows[at] + dot3(g_h[at], g_l[at], th[T:, :], tl[T:, :])

    last_block(far_rows)
    west, east = exists(0, -1), exists(0, 1)
    ends = [
        (gives, takes, gw.at[far_rows, mid], ecen, device(step, 0)),
        (jnp.logical_and(gives, west), jnp.logical_and(takes, east), gw.at[far_rows, low], eside.at[0], device(step, -1)),
        (jnp.logical_and(gives, east), jnp.logical_and(takes, west), gw.at[far_rows, high], eside.at[1], device(step, 1)),
        (west, east, gw.at[near_rows, low], eside.at[2], device(0, -1)),
        (east, west, gw.at[near_rows, high], eside.at[3], device(0, 1)),
    ]
    hops = [remote(src, dst, ess.at[n], ers.at[n], to) for n, (_, _, src, dst, to) in enumerate(ends)]
    for n in range(3):
        pl.when(ends[n][0])(hops[n].start)
    last_block(near_rows)
    for n in range(3, 5):
        pl.when(ends[n][0])(hops[n].start)
    lane = lax.broadcasted_iota(jnp.int32, (1, T), 1) // 64
    pixels = jnp.zeros((1, T), F32)
    for k in range(4):
        pixels = jnp.where(lane == k, active[j, k].astype(F32), pixels)
    pixels = pixels * SCALE
    for n in range(5):
        pl.when(ends[n][1])(hops[n].wait_recv)
    own_part = gw[near_rows, mid] + ecen[...]
    gradient[:, :R] = (own_part[:, :R] + eside[1] + eside[3]) * pixels[:, :R]
    gradient[:, R:] = (own_part[:, R:] + eside[0] + eside[2]) * pixels[:, R:]


    for n in range(8):
        pl.when(exists(*pieces[n][:2]))(copies[n].wait_send)
    for n in range(2):
        for d in range(3):
            pl.when(exists(-pieces[n][0], 0))(passes[d][n].wait_send)
    for copy in sums + shares + firsts + seconds:
        copy.wait_send()
    for n in range(5):
        pl.when(ends[n][0])(hops[n].wait_send)


def local(photomask, target_bits, active_blocks, kernel_taps, kernel_weights):
    hbm = pl.BlockSpec(memory_space=pl.ANY)
    smem = pl.BlockSpec(memory_space=pltpu.SMEM)
    vmem = pltpu.VMEM
    dma = pltpu.SemaphoreType.DMA
    scratch = [
        vmem((W, W), F32),
        vmem((2, 3, 2 * R + 1, 2 * R + 1), F32),
        vmem((W, W), BF), vmem((W, W), BF), vmem((W, W), BF), vmem((W, W), BF),
        vmem((T, T), jnp.int32),
        vmem((8, T), F32),
        vmem((8, W), F32),
        vmem((W, W), BF), vmem((W, W), BF),
        vmem((W, W), F32),
        vmem((PARTS, 4, T, T), F32),
        vmem((4, T, T), F32),
        vmem((PARTS, T, W), BF), vmem((PARTS, T, W), BF),
        vmem((PARTS, T, T), F32),
        vmem((PARTS, T, W), BF), vmem((PARTS, T, W), BF),
        vmem((8, Q, R), F32), vmem((8, Q, R), F32), vmem((8, Q, R), F32), vmem((8, Q, R), F32),
        vmem((4, T, R), F32),
        vmem((4, 4, 2, Q, R), F32),
        vmem((8, 2, Q, R), F32), vmem((4, 2, Q, R), F32), vmem((4, 2, Q, R), F32),
        vmem((2 * Q, W), F32),
        vmem((Q, T), F32), vmem((4, Q, R), F32),
        dma((14,)), dma((8,)), dma((8,)),
        dma((6,)), dma((6,)),
        dma((8,)), dma((8,)), dma((8,)), dma((8,)),
        dma((8,)), dma((8,)), dma((4,)), dma((4,)),
        dma((5,)), dma((5,)),
    ]
    return pl.pallas_call(
        kernel,
        out_shape=(vmem((Q, T), F32), vmem((T, T), F32)),
        in_specs=[hbm, hbm, smem, hbm, smem, hbm, hbm, hbm, hbm],
        out_specs=(pl.BlockSpec(memory_space=vmem), pl.BlockSpec(memory_space=vmem)),
        scratch_shapes=scratch,
        compiler_params=pltpu.CompilerParams(
            collective_id=0, has_side_effects=True, vmem_limit_bytes=56 * 1024 * 1024),
        name="socs",
    )(photomask, target_bits, active_blocks, kernel_taps.transpose(1, 2, 0, 3), kernel_weights,
      *[jnp.asarray(t) for t in tables()])


def solution(mesh):
    in_specs = (
        P("row", "col"),
        P("row", "col"),
        P("row", "col"),
        P(None, "kern", None, None),
        P("kern"),
    )
    out_specs = (P(("row", "kern"), "col"), P("row", "col"))
    return jax.shard_map(local, mesh=mesh, in_specs=in_specs, out_specs=out_specs, check_vma=False)
```
